512 devices in a mesh: row: 32 (over z, core), col: 16 (over y, x).
Axes of the slice: x: 4, y: 4, z: 16, core: 2. Of those that a mesh axis runs over, the one named last changes fastest.
Arguments:
- solved: float32 [2, 32768, 512], P(None, 'row'), may hold values from -6 to 6
- upper_cols: float32 [2, 2, 1024, 32768], P(None, None, 'col', 'row'), may hold values from -0.0234375 to 0.0234375
- coupling: float32 [2, 1024, 1024], P(None, 'col', 'row'), may hold values from -0.125 to 0.125
- inverse_diag: float32 [2, 2, 1024, 1024], P(None, None, 'row', 'col'), may hold values from -0.1875 to 0.1875
- right_side: float32 [2, 2, 1024, 512], P(None, None, 'col'), may hold values from -6 to 6
Outputs:
- answers: float32 [2, 2, 1024, 512], P(None, None, 'row')
The draws below stay inside these ranges and needn't reach their ends.
All inputs are finite; a program needn't handle non-finite values.
Results may differ from the reference program's by a relative error of at most 0.000082.
Values sent between devices are 32-bit elements; how exact they have to be, the bound alone decides.
A program may use at most 64 MiB of HBM per device.

```python
import jax
import jax.numpy as jnp
from jax import lax

PANEL = 1024
NRHS = 512
SOLVED = 32768


def levels(rng, dims, shards, low, top_value):
    factor_of = 1.0
    for position, shards_of in shards:
        heights = jax.random.uniform(jax.random.fold_in(jax.random.fold_in(rng, 6), position), (shards_of,), jnp.float32, low / len(shards), top_value / len(shards))
        factor_of = factor_of * jnp.repeat(jnp.exp(heights), dims[position] // shards_of).reshape((-1,) + (1,) * (len(dims) - 1 - position))
    return factor_of


def normal_values(own_key, shape, scale, reach, shards=(), kind=jnp.bfloat16):
    array = jax.random.normal(own_key, shape, jnp.float32) * scale
    if len(shards) > 0:
        array = levels(own_key, shape, shards, -0.22, 0.18) * array
    return jnp.clip(array, min=-reach, max=reach).astype(kind)


def setup_inputs(seed: int = 0) -> dict:
    streams_of = jax.random.split(jax.random.key(seed), 6)
    solved = normal_values(streams_of[0], (2, SOLVED, NRHS), 1.0, 6.0, ((1, 32),), jnp.float32)
    upper_cols = normal_values(streams_of[1], (2, 2, PANEL, SOLVED), (2 * SOLVED) ** -0.5, 0.0234375, ((2, 16), (3, 32)), jnp.float32)
    coupling = normal_values(streams_of[2], (2, PANEL, PANEL), (2 * PANEL) ** -0.5, 0.125, ((1, 16), (2, 32)), jnp.float32)
    inverse_diag = normal_values(streams_of[3], (2, 2, PANEL, PANEL), PANEL ** -0.5, 0.1875, ((2, 32), (3, 16)), jnp.float32)
    right_side = normal_values(streams_of[4], (2, 2, PANEL, NRHS), 1.0, 6.0, ((2, 16),), jnp.float32)
    return dict(solved=solved, upper_cols=upper_cols, coupling=coupling, inverse_diag=inverse_diag, right_side=right_side)


HIGHEST = lax.Precision.HIGHEST


def conj_apply(factor, vector):
    parts = jnp.einsum("smk,tkn->stmn", factor, vector, precision=HIGHEST)
    return jnp.stack([parts[0, 0] + parts[1, 1], parts[0, 1] - parts[1, 0]])


def complex_apply(matrix, vector):
    parts = jnp.einsum("smk,tkn->stmn", matrix, vector, precision=HIGHEST)
    return jnp.stack([parts[0, 0] - parts[1, 1], parts[0, 1] + parts[1, 0]])


def reference(solved, upper_cols, coupling, inverse_diag, right_side):
    prior_first = conj_apply(upper_cols[:, 0], solved)
    prior_second = conj_apply(upper_cols[:, 1], solved)
    answer_first = complex_apply(jnp.tril(inverse_diag[:, 0]), right_side[:, 0] - prior_first)
    coupled = conj_apply(coupling, answer_first)
    answer_second = complex_apply(jnp.tril(inverse_diag[:, 1]), right_side[:, 1] - (prior_second + coupled))
    return jnp.stack([answer_first, answer_second], axis=1)
```

```python
import functools

import jax
import jax.numpy as jnp
from jax import lax
from jax.experimental import pallas as pl
from jax.experimental.pallas import tpu as pltpu
from jax.sharding import PartitionSpec as P

MESH = pl.DeviceIdType.MESH
F32 = jnp.float32
BF16 = jnp.bfloat16
NZ = 16
NC = 16
KSTEP = 256

Z_PRIOR, Z_CPL, Z_Q, Z_ANS = 0, 2, 3, 5
C_ANS, C_U, C_UALL, C_OUT = 0, 2, 3, 4
K_PRIOR, K_CPL, K_Q, K_ANS = 0, 2, 3, 5


def split(x):
    hi = x.astype(BF16)
    return hi, (x - hi.astype(F32)).astype(BF16)


def dot3(a, b):
    (ah, al), (bh, bl) = a, b
    dot = functools.partial(jnp.dot, preferred_element_type=F32)
    return dot(ah, bh) + (dot(ah, bl) + dot(al, bh))


def tile(i, size):
    return pl.ds(pl.multiple_of(i * size, size), size)


def far_first(t):
    half = (t + 1) // 2
    return 8 + jnp.where(lax.rem(t, 2) == 1, -half, half)


def kernel(
    s_hbm, u_hbm, rs_hbm, w_ref, ct_ref, o_ref,
    a_buf, s_buf, x_buf, pt, cx, p2, rb, rsb, rst, wh, wl, qa, cg, pu, ru, ug, ubh, ubl, pp, rc, ga, ob,
    load_sem, zs, zr, cs, cr, ks, kr,
):
    row = lax.axis_index("row")
    c = lax.axis_index("col")
    z, k = row // 2, lax.rem(row, 2)
    ok = 1 - k

    def z_dev(i):
        return (lax.rem(z + i, NZ) * 2 + k, c)

    def c_dev(i):
        return (row, lax.rem(c + i, NC))

    sibling = (z * 2 + ok, c)

    barrier = pltpu.get_barrier_semaphore()
    pl.semaphore_signal(barrier, inc=1, device_id=sibling, device_id_type=MESH)

    def greet(t, _):
        i = far_first(t)
        pl.semaphore_signal(barrier, inc=1, device_id=z_dev(i), device_id_type=MESH)
        pl.semaphore_signal(barrier, inc=1, device_id=c_dev(i), device_id_type=MESH)
        return 0

    lax.fori_loop(0, NZ - 1, greet, 0)

    def remote(src, dst, ssem, rsem, dev):
        return pltpu.make_async_remote_copy(
            src_ref=src, dst_ref=dst, send_sem=ssem, recv_sem=rsem, device_id=dev, device_id_type=MESH
        )

    def z_send(g, src, dst):
        def body(t, _):
            i = far_first(t)
            remote(src(lax.rem(z + i, NZ)), dst(z), zs.at[g, i], zr.at[g, i], z_dev(i)).start()
            return 0

        lax.fori_loop(0, NZ - 1, body, 0)

    def z_wait(g, i, src, dst):
        frm = lax.rem(z - i + NZ, NZ)
        remote(src(frm), dst(frm), zs.at[g, i], zr.at[g, i], z_dev(i)).wait_recv()
        return frm

    def z_wait_all(g, src, dst):
        def body(i, _):
            z_wait(g, i, src, dst)
            return 0

        lax.fori_loop(1, NZ, body, 0)

    def c_send(g, src, dst):
        def body(t, _):
            i = far_first(t)
            remote(src(lax.rem(c + i, NC)), dst(c), cs.at[g, i], cr.at[g, i], c_dev(i)).start()
            return 0

        lax.fori_loop(0, NC - 1, body, 0)

    def c_wait(g, i, src, dst):
        frm = lax.rem(c - i + NC, NC)
        remote(src(frm), dst(frm), cs.at[g, i], cr.at[g, i], c_dev(i)).wait_recv()
        return frm

    def c_wait_all(g, src, dst):
        def body(i, _):
            c_wait(g, i, src, dst)
            return 0

        lax.fori_loop(1, NC, body, 0)

    def k_copy(g, src, dst):
        return remote(src, dst, ks.at[g], kr.at[g], sibling)

    loads_a = [
        pltpu.make_async_copy(u_hbm.at[s, p], a_buf.at[pl.ds((p * 2 + s) * 64, 64)], load_sem.at[p * 2 + s])
        for p in range(2)
        for s in range(2)
    ]

    def load_s(s, j):
        return pltpu.make_async_copy(
            s_hbm.at[s, tile(j, KSTEP)], s_buf.at[s, tile(j, KSTEP)], load_sem.at[8 + s * 4 + j]
        )

    block = k * 2 + z // 8
    loads_r = [
        pltpu.make_async_copy(
            rs_hbm.at[s, p, :, tile(block, 128)], rsb.at[p, pl.ds(s * 64, 64)], load_sem.at[4 + p * 2 + s]
        )
        for p in range(2)
        for s in range(2)
    ]
    for copy in loads_a:
        copy.start()
    for j in range(4):
        load_s(0, j).start()
        load_s(1, j).start()
    for copy in loads_r:
        copy.start()

    for copy in loads_a:
        copy.wait()

    def prior_step(j, _):
        a = split(a_buf[:, tile(j, KSTEP)])
        for s in range(2):
            load_s(s, j).wait()
            part = dot3(a, split(s_buf[s, tile(j, KSTEP), :]))

            @pl.when(j == 0)
            def _():
                x_buf[s] = part

            @pl.when(j > 0)
            def _():
                x_buf[s] += part

        return 0

    lax.fori_loop(0, 4, prior_step, 0)
    for p in range(2):
        lo, mid, hi = p * 128, p * 128 + 64, p * 128 + 128
        re = x_buf[0, lo:mid] + x_buf[1, mid:hi]
        im = x_buf[1, lo:mid] - x_buf[0, mid:hi]
        pt[p] = jnp.concatenate([re, im], axis=0).T
    for copy in loads_r:
        copy.wait()
    for p in range(2):
        rst[p] = rsb[p].T
        wh[p], wl[p] = split(w_ref[p])
    own_ct = cg.at[tile(z, 32), tile(k, 128)]
    own_ct[...] = ct_ref[...]

    pl.semaphore_wait(barrier, 1 + (NZ - 1) + (NC - 1))

    for p in range(2):
        k_copy(K_PRIOR + p, pt.at[p, tile(ok, 256)], cx.at[p]).start()
    for p in range(2):
        k_copy(K_PRIOR + p, pt.at[p, tile(ok, 256)], cx.at[p]).wait_recv()
        p2[p] = pt[p, tile(k, 256)] + cx[p]
        z_send(Z_PRIOR + p, lambda i: p2.at[p, tile(i, 16)], lambda i: rb.at[p, tile(i, 16)])
    z_send(Z_CPL, lambda i: own_ct, lambda i: cg.at[tile(i, 32), tile(k, 128)])

    for p in range(2):

        def arrived(i, total):
            frm = z_wait(Z_PRIOR + p, i, lambda i: p2.at[p, tile(i, 16)], lambda i: rb.at[p, tile(i, 16)])
            return total + rb[p, tile(frm, 16)]

        total = lax.fori_loop(1, NZ, arrived, p2[p, tile(z, 16)])
        own_q = qa.at[p, tile(z, 16), tile(k, 128)]
        own_q[...] = rst[p, tile(lax.rem(z, 8), 16)] - total
        z_send(Z_Q + p, lambda i: own_q, lambda i: qa.at[p, tile(i, 16), tile(k, 128)])

    z_wait_all(Z_CPL, lambda i: own_ct, lambda i: cg.at[tile(i, 32), tile(k, 128)])
    half = cg.at[:, tile(k, 128)]
    k_copy(K_CPL, half, half).start()
    k_copy(K_CPL, half, cg.at[:, tile(ok, 128)]).wait_recv()
    pu[...] = dot3(split(cg[...]), (wh[1], wl[1]))
    c_send(C_U, lambda i: pu.at[tile(i, 32)], lambda i: ru.at[tile(i, 32)])

    def lower(p):
        z_wait_all(Z_Q + p, lambda i: qa.at[p, tile(z, 16), tile(k, 128)], lambda i: qa.at[p, tile(i, 16), tile(k, 128)])
        half = qa.at[p, :, tile(k, 128)]
        k_copy(K_Q + p, half, half).start()
        k_copy(K_Q + p, half, qa.at[p, :, tile(ok, 128)]).wait_recv()
        pp[p] = dot3(split(qa[p]), (wh[p], wl[p]))
        c_send(C_ANS + p, lambda i: pp.at[p, tile(i, 16)], lambda i: rc.at[p, tile(i, 16)])

    def summed(p):
        def arrived(i, total):
            frm = c_wait(C_ANS + p, i, lambda i: pp.at[p, tile(i, 16)], lambda i: rc.at[p, tile(i, 16)])
            return total + rc[p, tile(frm, 16)]

        return lax.fori_loop(1, NC, arrived, pp[p, tile(c, 16)])

    def share(p, answer):
        own = ob.at[p, tile(c, 16)]
        own[...] = answer
        c_send(C_OUT + p, lambda i: own, lambda i: ob.at[p, tile(i, 16)])

    lower(0)

    def u_arrived(i, total):
        frm = c_wait(C_U, i, lambda i: pu.at[tile(i, 32)], lambda i: ru.at[tile(i, 32)])
        return total + ru[tile(frm, 32)]

    own_u = ug.at[tile(c, 32)]
    own_u[...] = lax.fori_loop(1, NC, u_arrived, pu[tile(c, 32)])
    c_send(C_UALL, lambda i: own_u, lambda i: ug.at[tile(i, 32)])

    answer_0 = summed(0)
    slot = k * NZ
    own_a = ga.at[:, tile(slot + z, 128)]
    own_a[...] = answer_0
    z_send(Z_ANS, lambda i: own_a, lambda i: ga.at[:, tile(slot + i, 128)])
    share(0, answer_0)

    lower(1)

    c_wait_all(C_UALL, lambda i: own_u, lambda i: ug.at[tile(i, 32)])
    lane = lax.broadcasted_iota(jnp.int32, (32, 128), 1)
    left = lane < 64
    imag = lax.rem(lane // 32, 2) == 1

    def weigh(i, _):
        v = ug[tile(i, 32)]
        v2 = jnp.where(imag, pltpu.roll(v, 32, 1), -pltpu.roll(v, 96, 1))
        t, t2 = pltpu.roll(v, 64, 1), pltpu.roll(v2, 64, 1)
        zero = jnp.zeros_like(v)
        for par, parts in enumerate([(v, v2, t, t2), (t, t2, v, v2)]):
            rows = jnp.concatenate(
                [
                    jnp.where(left, parts[0], zero),
                    jnp.where(left, parts[1], zero),
                    jnp.where(left, zero, parts[2]),
                    jnp.where(left, zero, parts[3]),
                ],
                axis=0,
            )
            hi, lo = split(rows)
            ubh[tile(par * NZ + i, 128)] = hi
            ubl[tile(par * NZ + i, 128)] = lo
        return 0

    lax.fori_loop(0, NC, weigh, 0)
    own_1 = summed(1)

    z_wait_all(Z_ANS, lambda i: own_a, lambda i: ga.at[:, tile(slot + i, 128)])
    half_a = ga.at[:, tile(k, NZ * 128)]
    k_copy(K_ANS, half_a, half_a).start()
    k_copy(K_ANS, half_a, ga.at[:, tile(ok, NZ * 128)]).wait_recv()
    share(1, own_1 - dot3(split(ga[...]), (ubh[...], ubl[...])))

    for p in range(2):
        c_wait_all(C_OUT + p, lambda i: ob.at[p, tile(c, 16)], lambda i: ob.at[p, tile(i, 16)])
        turned = ob[p].T
        for h in range(2):
            for s in range(2):
                at = (h * 2 + s) * 32
                o_ref[s, p, :, pl.ds(h * 256, 256)] = turned[at : at + 32]

    def drain(i, _):
        blk, big, act = rb.at[0, pl.ds(0, 16)], ru.at[pl.ds(0, 32)], ga.at[:, pl.ds(0, 128)]
        q = qa.at[0, pl.ds(0, 16), pl.ds(0, 128)]
        ctb = cg.at[pl.ds(0, 32), pl.ds(0, 128)]
        for g, ref in ((0, blk), (1, blk), (2, ctb), (3, q), (4, q), (5, act)):
            remote(ref, ref, zs.at[g, i], zr.at[g, i], z_dev(i)).wait_send()
        for g, ref in ((0, blk), (1, blk), (2, big), (3, big), (4, blk), (5, blk)):
            remote(ref, ref, cs.at[g, i], cr.at[g, i], c_dev(i)).wait_send()
        return 0

    lax.fori_loop(1, NZ, drain, 0)
    k_copy(0, cx.at[0], cx.at[0]).wait_send()
    k_copy(1, cx.at[1], cx.at[1]).wait_send()
    k_copy(2, half, half).wait_send()
    for p in range(2):
        hq = qa.at[p, :, tile(k, 128)]
        k_copy(K_Q + p, hq, hq).wait_send()
    k_copy(K_ANS, half_a, half_a).wait_send()


def per_device(solved, upper_cols, coupling, inverse_diag, right_side):
    rows, cols = inverse_diag.shape[2], inverse_diag.shape[3]
    row_global = lax.axis_index("row") * rows + jnp.arange(rows, dtype=jnp.int32)
    col_global = lax.axis_index("col") * cols + jnp.arange(cols, dtype=jnp.int32)
    low = jnp.where(col_global[None, :] <= row_global[:, None], inverse_diag, 0.0)
    re, im = jnp.swapaxes(low[0], 1, 2), jnp.swapaxes(low[1], 1, 2)
    w = jnp.concatenate([jnp.concatenate([re, im], 2), jnp.concatenate([-im, re], 2)], 1)
    none = jnp.zeros_like(w)
    w = jnp.concatenate([jnp.concatenate([w, none], 2), jnp.concatenate([none, w], 2)], 1)
    ct = jnp.concatenate([coupling[0].T, -coupling[1].T], 1)
    vmem = pl.BlockSpec(memory_space=pltpu.VMEM)
    hbm = pl.BlockSpec(memory_space=pltpu.HBM)
    f = lambda *shape: pltpu.VMEM(shape, F32)
    b = lambda *shape: pltpu.VMEM(shape, BF16)
    return pl.pallas_call(
        kernel,
        out_shape=jax.ShapeDtypeStruct((2, 2, 32, 512), F32),
        in_specs=[hbm, hbm, hbm, vmem, vmem],
        out_specs=vmem,
        scratch_shapes=[
            f(256, 1024), f(2, 1024, 512), f(2, 256, 512), f(2, 512, 128), f(2, 256, 128), f(2, 256, 128),
            f(2, 256, 128), f(2, 128, 128), f(2, 128, 128), b(2, 256, 128), b(2, 256, 128), f(2, 256, 256),
            f(512, 256), f(512, 128), f(512, 128), f(512, 128), b(4096, 128), b(4096, 128), f(2, 256, 128),
            f(2, 256, 128), f(16, 4096), f(2, 256, 128),
            pltpu.SemaphoreType.DMA((16,)),
            pltpu.SemaphoreType.DMA((6, 16)), pltpu.SemaphoreType.DMA((6, 16)),
            pltpu.SemaphoreType.DMA((6, 16)), pltpu.SemaphoreType.DMA((6, 16)),
            pltpu.SemaphoreType.DMA((6,)), pltpu.SemaphoreType.DMA((6,)),
        ],
        compiler_params=pltpu.CompilerParams(
            collective_id=0, has_side_effects=True, vmem_limit_bytes=48 * 1024 * 1024
        ),
        name="panels",
    )(solved, upper_cols, right_side, w, ct)


def solution(mesh):
    in_specs = (
        P(None, "row", None),
        P(None, None, "col", "row"),
        P(None, "col", "row"),
        P(None, None, "row", "col"),
        P(None, None, "col", None),
    )
    out_specs = P(None, None, "row", None)
    return jax.shard_map(
        per_device, mesh=mesh, in_specs=in_specs, out_specs=out_specs, check_vma=False
    )
```

```python
import functools

import jax
import jax.numpy as jnp
from jax import lax
from jax.experimental import pallas as pl
from jax.experimental.pallas import tpu as pltpu
from jax.sharding import PartitionSpec as P

MESH = pl.DeviceIdType.MESH
F32 = jnp.float32
BF16 = jnp.bfloat16
NZ = 16
NC = 16
KSTEP = 512
VMEM = 62 * 1024 * 1024

Z_PRIOR, Z_CPL, Z_Q, Z_ANS, Z_CPL2 = 0, 2, 3, 5, 6
C_ANS, C_U, C_UALL, C_OUT = 0, 2, 3, 4
K_PRIOR, K_INV, K_OUT, K_U = 0, 2, 3, 5


def split(x):
    hi = x.astype(BF16)
    return hi, (x - hi.astype(F32)).astype(BF16)


def dot3(a, b):
    (ah, al), (bh, bl) = a, b
    dot = functools.partial(jnp.dot, preferred_element_type=F32)
    return dot(ah, bh) + (dot(ah, bl) + dot(al, bh))


def tile(i, size):
    return pl.ds(i * size if isinstance(i, int) else pl.multiple_of(i * size, size), size)


def far_first(t):
    half = (t + 1) // 2
    return 8 + jnp.where(lax.rem(t, 2) == 1, -half, half)


def place(z):
    return lax.rem(z, 4) * 4 + z // 4


def kernel(
    s_hbm, u_hbm, rs_hbm, d_hbm, c_hbm, o_ref,
    d_buf, c_buf, a_buf, s_buf, x_buf, pt, cx, p2, rb, rsb, rst, wh, wl, qa, cg, pu, ru, ug, ubh, ubl, pp, rc, ga, xb, xs, ob,
    load_sem, zs, zr, cs, cr, ks, kr,
):
    row = lax.axis_index("row")
    c = lax.axis_index("col")
    z, k = row // 2, lax.rem(row, 2)
    ok = 1 - k

    def z_dev(i):
        return (lax.rem(z + i, NZ) * 2 + k, c)

    def c_dev(i):
        return (row, lax.rem(c + i, NC))

    sibling = (z * 2 + ok, c)

    barrier = pltpu.get_barrier_semaphore()
    pl.semaphore_signal(barrier, inc=1, device_id=sibling, device_id_type=MESH)

    def greet(t, _):
        i = far_first(t)
        pl.semaphore_signal(barrier, inc=1, device_id=z_dev(i), device_id_type=MESH)
        pl.semaphore_signal(barrier, inc=1, device_id=c_dev(i), device_id_type=MESH)
        return 0

    lax.fori_loop(0, NZ - 1, greet, 0)

    def remote(src, dst, ssem, rsem, dev):
        return pltpu.make_async_remote_copy(
            src_ref=src, dst_ref=dst, send_sem=ssem, recv_sem=rsem, device_id=dev, device_id_type=MESH
        )

    def z_send(g, src, dst):
        def body(t, _):
            i = far_first(t)
            remote(src(lax.rem(z + i, NZ)), dst(z), zs.at[g, i], zr.at[g, i], z_dev(i)).start()
            return 0

        lax.fori_loop(0, NZ - 1, body, 0)

    def z_wait(g, i, src, dst):
        frm = lax.rem(z - i + NZ, NZ)
        remote(src(frm), dst(frm), zs.at[g, i], zr.at[g, i], z_dev(i)).wait_recv()
        return frm

    def z_wait_all(g, src, dst):
        def body(i, _):
            z_wait(g, i, src, dst)
            return 0

        lax.fori_loop(1, NZ, body, 0)

    def c_send(g, src, dst):
        def body(t, _):
            i = far_first(t)
            remote(src(lax.rem(c + i, NC)), dst(c), cs.at[g, i], cr.at[g, i], c_dev(i)).start()
            return 0

        lax.fori_loop(0, NC - 1, body, 0)

    def c_wait(g, i, src, dst):
        frm = lax.rem(c - i + NC, NC)
        remote(src(frm), dst(frm), cs.at[g, i], cr.at[g, i], c_dev(i)).wait_recv()
        return frm

    def c_wait_all(g, src, dst):
        def body(i, _):
            c_wait(g, i, src, dst)
            return 0

        lax.fori_loop(1, NC, body, 0)

    def k_copy(g, src, dst):
        return remote(src, dst, ks.at[g], kr.at[g], sibling)

    loads_a = [
        pltpu.make_async_copy(u_hbm.at[s, p], a_buf.at[pl.ds((p * 2 + s) * 64, 64)], load_sem.at[p * 2 + s])
        for p in range(2)
        for s in range(2)
    ]

    def load_s(s, j):
        return pltpu.make_async_copy(
            s_hbm.at[s, tile(j, KSTEP)], s_buf.at[s, tile(j, KSTEP)], load_sem.at[8 + s * 4 + j]
        )

    block = k * 2 + z // 8
    loads_r = [
        pltpu.make_async_copy(
            rs_hbm.at[s, p, :, tile(block, 128)], rsb.at[p, pl.ds(s * 64, 64)], load_sem.at[4 + p * 2 + s]
        )
        for p in range(2)
        for s in range(2)
    ]
    loads_r.append(pltpu.make_async_copy(d_hbm, d_buf.at[k], load_sem.at[16]))
    loads_r.append(pltpu.make_async_copy(c_hbm, c_buf, load_sem.at[17]))
    for copy in loads_a:
        copy.start()
    for j in range(1024 // KSTEP):
        load_s(0, j).start()
        load_s(1, j).start()
    for copy in loads_r:
        copy.start()

    for copy in loads_a:
        copy.wait()

    def prior_step(j, _):
        a = split(a_buf[:, tile(j, KSTEP)])
        for s in range(2):
            load_s(s, j).wait()
            part = dot3(a, split(s_buf[s, tile(j, KSTEP), :]))

            if j == 0:
                x_buf[s] = part
            else:
                x_buf[s] += part

    for j in range(1024 // KSTEP):
        prior_step(j, 0)
    for copy in loads_r:
        copy.wait()
    own_ct = cg.at[tile(place(z), 32)]
    own_ct[...] = jnp.concatenate([c_buf[0], -c_buf[1]], 1)

    pl.semaphore_wait(barrier, 1 + (NZ - 1) + (NC - 1))

    def cpl_copy(i):
        return remote(own_ct, own_ct, zs.at[Z_CPL, i], zr.at[Z_CPL, i], z_dev(i))

    for i in (8, 4, 12):
        cpl_copy(i).start()
    own_d = d_buf.at[k]
    k_copy(K_INV, own_d, own_d).start()

    for p in range(2):
        lo, mid, hi = p * 128, p * 128 + 64, p * 128 + 128
        re = x_buf[0, lo:mid] + x_buf[1, mid:hi]
        im = x_buf[1, lo:mid] - x_buf[0, mid:hi]
        pt[p] = jnp.concatenate([re, im], axis=0).T
        k_copy(K_PRIOR + p, pt.at[p, tile(ok, 256)], cx.at[p]).start()
    for p in range(2):
        k_copy(K_PRIOR + p, pt.at[p, tile(ok, 256)], cx.at[p]).wait_recv()
        p2[p] = pt[p, tile(k, 256)] + cx[p]
        z_send(Z_PRIOR + p, lambda i: p2.at[p, tile(i, 16)], lambda i: rb.at[p, tile(i, 16)])
    for p in range(2):
        rst[p] = rsb[p].T
    k_copy(K_INV, own_d, d_buf.at[ok]).wait_recv()
    at = lax.broadcasted_iota(jnp.int32, (32, 64), 0) - lax.broadcasted_iota(jnp.int32, (32, 64), 1)
    for p in range(2):
        lines = []
        for q in range(2):
            low = c * 64 <= at + (z * 64 + q * 32)
            re, im = (jnp.where(low, d_buf[q, s, p], 0.0) for s in range(2))
            lines += [jnp.concatenate([re, -im], 1), jnp.concatenate([im, re], 1)]
        wh[p], wl[p] = split(jnp.concatenate(lines, 0).T)

    onward = ((0, 1, 0, 128), (1, -1, 0, 128), (2, 2, 0, 64), (3, -2, 64, 64))

    def onward_copy(n, step, first, rows, frm):
        ref = cg.at[pl.ds(pl.multiple_of(lax.rem(frm, 4) * 128 + first, 64), rows)]
        return remote(ref, ref, zs.at[Z_CPL2, n], zr.at[Z_CPL2, n], z_dev(step + NZ))

    for i in (4, 8, 12):
        cpl_copy(i).wait_recv()
    for n, step, first, rows in onward:
        onward_copy(n, step, first, rows, z).start()

    def gather_q(p):
        def arrived(i, total):
            frm = z_wait(Z_PRIOR + p, i, lambda i: p2.at[p, tile(i, 16)], lambda i: rb.at[p, tile(i, 16)])
            return total + rb[p, tile(frm, 16)]

        total = lax.fori_loop(1, NZ, arrived, p2[p, tile(z, 16)])
        own_q = qa.at[p, tile(z, 16)]
        own_q[...] = rst[p, tile(lax.rem(z, 8), 16)] - total
        z_send(Z_Q + p, lambda i: own_q, lambda i: qa.at[p, tile(i, 16)])

    gather_q(0)

    for n, step, first, rows in onward:
        onward_copy(n, step, first, rows, z - step + NZ).wait_recv()
    pu[...] = dot3(split(cg[...]), (wh[1], wl[1]))
    c_send(C_U, lambda i: pu.at[tile(i, 32)], lambda i: ru.at[tile(i, 32)])
    gather_q(1)

    def lower(p):
        z_wait_all(Z_Q + p, lambda i: qa.at[p, tile(z, 16)], lambda i: qa.at[p, tile(i, 16)])
        pp[p] = dot3(split(qa[p]), (wh[p], wl[p]))
        c_send(C_ANS + p, lambda i: pp.at[p, tile(i, 16)], lambda i: rc.at[p, tile(i, 16)])

    def summed(p):
        def arrived(i, total):
            frm = c_wait(C_ANS + p, i, lambda i: pp.at[p, tile(i, 16)], lambda i: rc.at[p, tile(i, 16)])
            return total + rc[p, tile(frm, 16)]

        return lax.fori_loop(1, NC, arrived, pp[p, tile(c, 16)])

    lane = lax.broadcasted_iota(jnp.int32, (16, 128), 1)
    own_lanes = lane // 64 == k

    def swap(p):
        return k_copy(K_OUT + p, xb.at[p], xs.at[p])

    def share(p):
        swap(p).wait_recv()
        own = ob.at[p, tile(c, 16)]
        own[...] = jnp.where(own_lanes, xb[p], pltpu.roll(xs[p], 64, 1))
        c_send(C_OUT + p, lambda i: own, lambda i: ob.at[p, tile(i, 16)])

    lower(0)

    def u_arrived(i, total):
        frm = c_wait(C_U, i, lambda i: pu.at[tile(i, 32)], lambda i: ru.at[tile(i, 32)])
        return total + ru[tile(frm, 32)]

    own_u = ug.at[k, tile(c, 32)]
    own_u[...] = lax.fori_loop(1, NC, u_arrived, pu[tile(c, 32)])
    c_send(C_UALL, lambda i: own_u, lambda i: ug.at[k, tile(i, 32)])

    own_a = ga.at[:, tile(z, 128)]
    answer_0 = summed(0)
    own_a[...] = answer_0
    z_send(Z_ANS, lambda i: own_a, lambda i: ga.at[:, tile(i, 128)])
    xb[0] = answer_0
    swap(0).start()

    lower(1)

    c_wait_all(C_UALL, lambda i: own_u, lambda i: ug.at[k, tile(i, 32)])
    half = ug.at[k]
    k_copy(K_U, half, half).start()
    share(0)

    k_copy(K_U, half, ug.at[ok]).wait_recv()
    imag = lax.rem(lax.broadcasted_iota(jnp.int32, (32, 128), 1) // 32, 2) == 1

    def weigh(i, _):
        for q in range(2):
            v = ug[q, tile(i, 32)]
            v2 = jnp.where(imag, pltpu.roll(v, 32, 1), -pltpu.roll(v, 96, 1))
            hi, lo = split(jnp.concatenate([v, v2], axis=0))
            ubh[tile(place(i) * 2 + q, 64)] = hi
            ubl[tile(place(i) * 2 + q, 64)] = lo
        return 0

    lax.fori_loop(0, NC, weigh, 0)
    own_1 = summed(1)

    z_wait_all(Z_ANS, lambda i: own_a, lambda i: ga.at[:, tile(i, 128)])
    xb[1] = own_1 - dot3(split(ga[...]), (ubh[...], ubl[...]))
    swap(1).start()
    share(1)

    for p in range(2):
        c_wait_all(C_OUT + p, lambda i: ob.at[p, tile(c, 16)], lambda i: ob.at[p, tile(i, 16)])
        turned = ob[p].T
        for h in range(2):
            for s in range(2):
                at = (h * 2 + s) * 32
                o_ref[s, p, :, pl.ds(h * 256, 256)] = turned[at : at + 32]

    def drain(i, _):
        blk, big, act = rb.at[0, pl.ds(0, 16)], ru.at[pl.ds(0, 32)], ga.at[:, pl.ds(0, 128)]
        q = qa.at[0, pl.ds(0, 16)]
        for g, ref in ((0, blk), (1, blk), (3, q), (4, q), (5, act)):
            remote(ref, ref, zs.at[g, i], zr.at[g, i], z_dev(i)).wait_send()
        for g, ref in ((0, blk), (1, blk), (2, big), (3, big), (4, blk), (5, blk)):
            remote(ref, ref, cs.at[g, i], cr.at[g, i], c_dev(i)).wait_send()
        return 0

    lax.fori_loop(1, NZ, drain, 0)
    for i in (4, 8, 12):
        cpl_copy(i).wait_send()
    for n, step, first, rows in onward:
        onward_copy(n, step, first, rows, z).wait_send()
    k_copy(0, cx.at[0], cx.at[0]).wait_send()
    k_copy(1, cx.at[1], cx.at[1]).wait_send()
    k_copy(K_INV, own_d, own_d).wait_send()
    k_copy(K_U, half, half).wait_send()
    for p in range(2):
        swap(p).wait_send()


def per_device(solved, upper_cols, coupling, inverse_diag, right_side):
    vmem = pl.BlockSpec(memory_space=pltpu.VMEM)
    hbm = pl.BlockSpec(memory_space=pltpu.HBM)
    f = lambda *shape: pltpu.VMEM(shape, F32)
    b = lambda *shape: pltpu.VMEM(shape, BF16)
    return pl.pallas_call(
        kernel,
        out_shape=pltpu.VMEM((2, 2, 32, 512), F32),
        in_specs=[hbm] * 5,
        out_specs=vmem,
        scratch_shapes=[
            f(2, 2, 2, 32, 64), f(2, 32, 64), f(256, 1024), f(2, 1024, 512), f(2, 256, 512), f(2, 512, 128),
            f(2, 256, 128), f(2, 256, 128), f(2, 256, 128), f(2, 128, 128), f(2, 128, 128),
            b(2, 128, 128), b(2, 128, 128), f(2, 256, 128), f(512, 128), f(512, 128), f(512, 128), f(2, 512, 128),
            b(2048, 128), b(2048, 128), f(2, 256, 128), f(2, 256, 128), f(16, 2048), f(2, 16, 128), f(2, 16, 128),
            f(2, 256, 128),
            pltpu.SemaphoreType.DMA((18,)),
            pltpu.SemaphoreType.DMA((7, 16)), pltpu.SemaphoreType.DMA((7, 16)),
            pltpu.SemaphoreType.DMA((6, 16)), pltpu.SemaphoreType.DMA((6, 16)),
            pltpu.SemaphoreType.DMA((6,)), pltpu.SemaphoreType.DMA((6,)),
        ],
        compiler_params=pltpu.CompilerParams(
            collective_id=0, has_side_effects=True, vmem_limit_bytes=VMEM
        ),
        name="panels",
    )(solved, upper_cols, right_side, inverse_diag, jnp.swapaxes(coupling, 1, 2))


def solution(mesh):
    in_specs = (
        P(None, "row", None),
        P(None, None, "col", "row"),
        P(None, "col", "row"),
        P(None, None, "row", "col"),
        P(None, None, "col", None),
    )
    out_specs = P(None, None, "row", None)
    return jax.shard_map(
        per_device, mesh=mesh, in_specs=in_specs, out_specs=out_specs, check_vma=False
    )
```

```python
import functools

import jax
import jax.numpy as jnp
from jax import lax
from jax.experimental import pallas as pl
from jax.experimental.pallas import tpu as pltpu
from jax.sharding import PartitionSpec as P

MESH = pl.DeviceIdType.MESH
F32 = jnp.float32
BF16 = jnp.bfloat16
NZ = 16
NC = 16
KSTEP = 512
VMEM = 62 * 1024 * 1024

Z_PRIOR, Z_CPL, Z_Q, Z_ANS, Z_CPL2 = 0, 2, 3, 5, 6
C_ANS, C_U, C_UALL, C_OUT = 0, 2, 3, 4
K_PRIOR, K_INV, K_OUT, K_U = 0, 2, 3, 5


def split(x):
    hi = x.astype(BF16)
    return hi, (x - hi.astype(F32)).astype(BF16)


def dot3(a, b):
    (ah, al), (bh, bl) = a, b
    dot = functools.partial(jnp.dot, preferred_element_type=F32)
    return dot(ah, bh) + (dot(ah, bl) + dot(al, bh))


def tile(i, size):
    return pl.ds(i * size if isinstance(i, int) else pl.multiple_of(i * size, size), size)


FAR_Z = (8, 7, 9, 6, 10, 5, 11, 4, 12, 3, 13, 2, 14, 1, 15)
FAR_C = (10, 9, 11, 6, 14, 5, 7, 13, 15, 8, 2, 1, 3, 4, 12)


def place(z):
    return lax.rem(z, 4) * 4 + z // 4


def kernel(
    s_hbm, u_hbm, rs_hbm, d_hbm, c_hbm, o_ref,
    d_buf, c_buf, a_buf, s_buf, x_buf, pt, cx, p2, rb, ra, pm, rf, rsb, rst, wh, wl, qa, cg, pu, ru, ug, ubh, ubl, pp, rc, ga, xb, xs, ob,
    load_sem, zs, zr, cs, cr, ks, kr,
):
    row = lax.axis_index("row")
    c = lax.axis_index("col")
    z, k = row // 2, lax.rem(row, 2)
    ok = 1 - k

    def z_dev(i):
        return (lax.rem(z + i, NZ) * 2 + k, c)

    def c_at(i):
        return lax.rem(c // 4 + i // 4, 4) * 4 + lax.rem(c + i, 4)

    def c_dev(i):
        return (row, c_at(i))

    sibling = (z * 2 + ok, c)

    barrier = pltpu.get_barrier_semaphore()
    pl.semaphore_signal(barrier, inc=1, device_id=sibling, device_id_type=MESH)

    for i, j in zip(FAR_Z, FAR_C):
        pl.semaphore_signal(barrier, inc=1, device_id=z_dev(i), device_id_type=MESH)
        pl.semaphore_signal(barrier, inc=1, device_id=c_dev(j), device_id_type=MESH)

    def remote(src, dst, ssem, rsem, dev):
        return pltpu.make_async_remote_copy(
            src_ref=src, dst_ref=dst, send_sem=ssem, recv_sem=rsem, device_id=dev, device_id_type=MESH
        )

    def z_send(g, src, dst):
        for i in FAR_Z:
            remote(src(lax.rem(z + i, NZ)), dst(z), zs.at[g, i], zr.at[g, i], z_dev(i)).start()

    def z_wait(g, i, src, dst):
        frm = lax.rem(z - i + NZ, NZ)
        remote(src(frm), dst(frm), zs.at[g, i], zr.at[g, i], z_dev(i)).wait_recv()
        return frm

    def z_wait_all(g, src, dst):
        def body(i, _):
            z_wait(g, i, src, dst)
            return 0

        lax.fori_loop(1, NZ, body, 0)

    def c_send(g, src, dst):
        for i in FAR_C:
            remote(src(c_at(i)), dst(c), cs.at[g, i], cr.at[g, i], c_dev(i)).start()

    def c_wait(g, i, src, dst):
        frm = lax.rem(c // 4 - i // 4 + 4, 4) * 4 + lax.rem(c - lax.rem(i, 4) + 4, 4)
        remote(src(frm), dst(frm), cs.at[g, i], cr.at[g, i], c_dev(i)).wait_recv()
        return frm

    def c_wait_all(g, src, dst):
        def body(i, _):
            c_wait(g, i, src, dst)
            return 0

        lax.fori_loop(1, NC, body, 0)

    def k_copy(g, src, dst):
        return remote(src, dst, ks.at[g], kr.at[g], sibling)

    loads_a = [
        pltpu.make_async_copy(u_hbm.at[s, p], a_buf.at[pl.ds((p * 2 + s) * 64, 64)], load_sem.at[p * 2 + s])
        for p in range(2)
        for s in range(2)
    ]

    def load_s(s, j):
        return pltpu.make_async_copy(
            s_hbm.at[s, tile(j, KSTEP)], s_buf.at[s, tile(j, KSTEP)], load_sem.at[8 + s * 4 + j]
        )

    block = k * 2 + z // 8
    loads_r = [
        pltpu.make_async_copy(
            rs_hbm.at[s, p, :, tile(block, 128)], rsb.at[p, pl.ds(s * 64, 64)], load_sem.at[4 + p * 2 + s]
        )
        for p in range(2)
        for s in range(2)
    ]
    loads_r.append(pltpu.make_async_copy(d_hbm, d_buf.at[k], load_sem.at[16]))
    loads_r.append(pltpu.make_async_copy(c_hbm, c_buf, load_sem.at[17]))
    for copy in loads_a:
        copy.start()
    for j in range(1024 // KSTEP):
        load_s(0, j).start()
        load_s(1, j).start()
    for copy in loads_r:
        copy.start()

    for copy in loads_a:
        copy.wait()

    def prior_step(j, _):
        a = split(a_buf[:, tile(j, KSTEP)])
        for s in range(2):
            load_s(s, j).wait()
            part = dot3(a, split(s_buf[s, tile(j, KSTEP), :]))

            if j == 0:
                x_buf[s] = part
            else:
                x_buf[s] += part

    for j in range(1024 // KSTEP):
        prior_step(j, 0)
    for copy in loads_r:
        copy.wait()
    own_ct = cg.at[tile(place(z), 32)]
    own_ct[...] = jnp.concatenate([c_buf[0], -c_buf[1]], 1)

    def cpl_copy(i):
        return remote(own_ct, own_ct, zs.at[Z_CPL, i], zr.at[Z_CPL, i], z_dev(i))

    pl.semaphore_wait(barrier, 1 + (NZ - 1) + (NC - 1))
    for i in (8, 4, 12):
        cpl_copy(i).start()


    for p in range(2):
        lo, mid, hi = p * 128, p * 128 + 64, p * 128 + 128
        re = x_buf[0, lo:mid] + x_buf[1, mid:hi]
        im = x_buf[1, lo:mid] - x_buf[0, mid:hi]
        pt[p] = jnp.concatenate([re, im], axis=0).T
        rst[p] = rsb[p].T


    for p in range(2):
        k_copy(K_PRIOR + p, pt.at[p, tile(ok, 256)], cx.at[p]).start()
    own_d = d_buf.at[k]
    k_copy(K_INV, own_d, own_d).start()

    for p in range(2):
        k_copy(K_PRIOR + p, pt.at[p, tile(ok, 256)], cx.at[p]).wait_recv()
        if p == 0:
            p2[0] = pt[0, tile(k, 256)] + cx[0]
            z_send(Z_PRIOR, lambda i: p2.at[0, tile(i, 16)], lambda i: rb.at[tile(i, 16)])
    for i in range(NZ):
        p2[1, tile(place(i), 16)] = pt[1, pl.ds(pl.multiple_of(k * 256 + i * 16, 16), 16)] + cx[1, tile(i, 16)]

    near = ((0, 1, 0, 0, 64), (1, -1, 1, 0, 64), (2, 2, 2, 0, 32), (3, -2, 2, 32, 32))

    def near_copy(n, step, to, first, rows):
        group = lax.rem(z + step + NZ, 4)
        src = p2.at[1, pl.ds(pl.multiple_of(group * 64 + first, 32), rows)]
        return remote(src, ra.at[to, pl.ds(first, rows)], zs.at[1, n], zr.at[1, n], z_dev(step + NZ))

    def fourth_copy(i):
        src = pm.at[tile(lax.rem(z + i, NZ) // 4, 16)]
        return remote(src, rf.at[i // 4], zs.at[1, i], zr.at[1, i], z_dev(i))

    for args in near:
        near_copy(*args).start()
    k_copy(K_INV, own_d, d_buf.at[ok]).wait_recv()
    at = lax.broadcasted_iota(jnp.int32, (32, 64), 0) - lax.broadcasted_iota(jnp.int32, (32, 64), 1)
    for p in range(2):
        lines = []
        for q in range(2):
            low = c * 64 <= at + (z * 64 + q * 32)
            re, im = (jnp.where(low, d_buf[q, s, p], 0.0) for s in range(2))
            lines += [jnp.concatenate([re, -im], 1), jnp.concatenate([im, re], 1)]
        wh[p], wl[p] = split(jnp.concatenate(lines, 0).T)

    onward = ((0, 1, 0, 128), (1, -1, 0, 128), (2, 2, 0, 64), (3, -2, 64, 64))

    def onward_copy(n, step, first, rows, frm):
        ref = cg.at[pl.ds(pl.multiple_of(lax.rem(frm, 4) * 128 + first, 64), rows)]
        return remote(ref, ref, zs.at[Z_CPL2, n], zr.at[Z_CPL2, n], z_dev(step + NZ))

    for i in (4, 8, 12):
        cpl_copy(i).wait_recv()
    for n, step, first, rows in onward:
        onward_copy(n, step, first, rows, z).start()

    for args in near:
        near_copy(*args).wait_recv()
    pm[...] = p2[1, tile(lax.rem(z, 4), 64)] + ra[0] + (ra[1] + ra[2])
    for i in (8, 4, 12):
        fourth_copy(i).start()

    def gather_q(p):
        def arrived(i, total):
            frm = z_wait(Z_PRIOR, i, lambda i: p2.at[0, tile(i, 16)], lambda i: rb.at[tile(i, 16)])
            return total + rb[tile(frm, 16)]

        if p == 0:
            total = lax.fori_loop(1, NZ, arrived, p2[0, tile(z, 16)])
        else:
            total = pm[tile(z // 4, 16)]
            for i in (4, 8, 12):
                fourth_copy(i).wait_recv()
                total = total + rf[i // 4]
        own_q = qa.at[p, tile(z, 16)]
        own_q[...] = rst[p, tile(lax.rem(z, 8), 16)] - total
        z_send(Z_Q + p, lambda i: own_q, lambda i: qa.at[p, tile(i, 16)])

    gather_q(0)

    for n, step, first, rows in onward:
        onward_copy(n, step, first, rows, z - step + NZ).wait_recv()
    pu[...] = dot3(split(cg[...]), (wh[1], wl[1]))
    c_send(C_U, lambda i: pu.at[tile(i, 32)], lambda i: ru.at[tile(i, 32)])
    gather_q(1)

    def lower(p):
        z_wait_all(Z_Q + p, lambda i: qa.at[p, tile(z, 16)], lambda i: qa.at[p, tile(i, 16)])
        pp[p] = dot3(split(qa[p]), (wh[p], wl[p]))
        c_send(C_ANS + p, lambda i: pp.at[p, tile(i, 16)], lambda i: rc.at[p, tile(i, 16)])

    def summed(p):
        def arrived(i, total):
            frm = c_wait(C_ANS + p, i, lambda i: pp.at[p, tile(i, 16)], lambda i: rc.at[p, tile(i, 16)])
            return total + rc[p, tile(frm, 16)]

        return lax.fori_loop(1, NC, arrived, pp[p, tile(c, 16)])

    lane = lax.broadcasted_iota(jnp.int32, (16, 128), 1)
    own_lanes = lane // 64 == k

    def swap(p):
        return k_copy(K_OUT + p, xb.at[p], xs.at[p])

    def share(p):
        swap(p).wait_recv()
        own = ob.at[p, tile(c, 16)]
        own[...] = jnp.where(own_lanes, xb[p], pltpu.roll(xs[p], 64, 1))
        c_send(C_OUT + p, lambda i: own, lambda i: ob.at[p, tile(i, 16)])

    lower(0)

    def u_arrived(i, total):
        frm = c_wait(C_U, i, lambda i: pu.at[tile(i, 32)], lambda i: ru.at[tile(i, 32)])
        return total + ru[tile(frm, 32)]

    own_u = ug.at[k, tile(c, 32)]
    own_u[...] = lax.fori_loop(1, NC, u_arrived, pu[tile(c, 32)])
    c_send(C_UALL, lambda i: own_u, lambda i: ug.at[k, tile(i, 32)])

    own_a = ga.at[:, tile(z, 128)]
    answer_0 = summed(0)
    own_a[...] = answer_0
    z_send(Z_ANS, lambda i: own_a, lambda i: ga.at[:, tile(i, 128)])
    xb[0] = answer_0
    swap(0).start()

    lower(1)

    c_wait_all(C_UALL, lambda i: own_u, lambda i: ug.at[k, tile(i, 32)])
    half = ug.at[k]
    k_copy(K_U, half, half).start()
    share(0)

    k_copy(K_U, half, ug.at[ok]).wait_recv()
    imag = lax.rem(lax.broadcasted_iota(jnp.int32, (32, 128), 1) // 32, 2) == 1

    def weigh(i, _):
        for q in range(2):
            v = ug[q, tile(i, 32)]
            v2 = jnp.where(imag, pltpu.roll(v, 32, 1), -pltpu.roll(v, 96, 1))
            hi, lo = split(jnp.concatenate([v, v2], axis=0))
            ubh[tile(place(i) * 2 + q, 64)] = hi
            ubl[tile(place(i) * 2 + q, 64)] = lo
        return 0

    lax.fori_loop(0, NC, weigh, 0)
    own_1 = summed(1)

    z_wait_all(Z_ANS, lambda i: own_a, lambda i: ga.at[:, tile(i, 128)])
    xb[1] = own_1 - dot3(split(ga[...]), (ubh[...], ubl[...]))
    swap(1).start()
    share(1)

    for p in range(2):
        c_wait_all(C_OUT + p, lambda i: ob.at[p, tile(c, 16)], lambda i: ob.at[p, tile(i, 16)])
        turned = ob[p].T
        for h in range(2):
            for s in range(2):
                at = (h * 2 + s) * 32
                o_ref[s, p, :, pl.ds(h * 256, 256)] = turned[at : at + 32]

    def drain(i, _):
        blk, big, act = rb.at[pl.ds(0, 16)], ru.at[pl.ds(0, 32)], ga.at[:, pl.ds(0, 128)]
        q = qa.at[0, pl.ds(0, 16)]
        for g, ref in ((0, blk), (3, q), (4, q), (5, act)):
            remote(ref, ref, zs.at[g, i], zr.at[g, i], z_dev(i)).wait_send()
        for g, ref in ((0, blk), (1, blk), (2, big), (3, big), (4, blk), (5, blk)):
            remote(ref, ref, cs.at[g, i], cr.at[g, i], c_dev(i)).wait_send()
        return 0

    lax.fori_loop(1, NZ, drain, 0)
    for i in (4, 8, 12):
        cpl_copy(i).wait_send()
        fourth_copy(i).wait_send()
    for args in near:
        near_copy(*args).wait_send()
    for n, step, first, rows in onward:
        onward_copy(n, step, first, rows, z).wait_send()
    k_copy(0, cx.at[0], cx.at[0]).wait_send()
    k_copy(1, cx.at[1], cx.at[1]).wait_send()
    k_copy(K_INV, own_d, own_d).wait_send()
    k_copy(K_U, half, half).wait_send()
    for p in range(2):
        swap(p).wait_send()


def per_device(solved, upper_cols, coupling, inverse_diag, right_side):
    vmem = pl.BlockSpec(memory_space=pltpu.VMEM)
    hbm = pl.BlockSpec(memory_space=pltpu.HBM)
    f = lambda *shape: pltpu.VMEM(shape, F32)
    b = lambda *shape: pltpu.VMEM(shape, BF16)
    return pl.pallas_call(
        kernel,
        out_shape=pltpu.VMEM((2, 2, 32, 512), F32),
        in_specs=[hbm] * 5,
        out_specs=vmem,
        scratch_shapes=[
            f(2, 2, 2, 32, 64), f(2, 32, 64), f(256, 1024), f(2, 1024, 512), f(2, 256, 512), f(2, 512, 128),
            f(2, 256, 128), f(2, 256, 128), f(256, 128), f(3, 64, 128), f(64, 128), f(4, 16, 128), f(2, 128, 128), f(2, 128, 128),
            b(2, 128, 128), b(2, 128, 128), f(2, 256, 128), f(512, 128), f(512, 128), f(512, 128), f(2, 512, 128),
            b(2048, 128), b(2048, 128), f(2, 256, 128), f(2, 256, 128), f(16, 2048), f(2, 16, 128), f(2, 16, 128),
            f(2, 256, 128),
            pltpu.SemaphoreType.DMA((18,)),
            pltpu.SemaphoreType.DMA((7, 16)), pltpu.SemaphoreType.DMA((7, 16)),
            pltpu.SemaphoreType.DMA((6, 16)), pltpu.SemaphoreType.DMA((6, 16)),
            pltpu.SemaphoreType.DMA((6,)), pltpu.SemaphoreType.DMA((6,)),
        ],
        compiler_params=pltpu.CompilerParams(
            collective_id=0, has_side_effects=True, vmem_limit_bytes=VMEM
        ),
        name="panels",
    )(solved, upper_cols, right_side, inverse_diag, jnp.swapaxes(coupling, 1, 2))


def solution(mesh):
    in_specs = (
        P(None, "row", None),
        P(None, None, "col", "row"),
        P(None, "col", "row"),
        P(None, None, "row", "col"),
        P(None, None, "col", None),
    )
    out_specs = P(None, None, "row", None)
    return jax.shard_map(
        per_device, mesh=mesh, in_specs=in_specs, out_specs=out_specs, check_vma=False
    )
```

```python
import functools

import jax
import jax.numpy as jnp
from jax import lax
from jax.experimental import pallas as pl
from jax.experimental.pallas import tpu as pltpu
from jax.sharding import PartitionSpec as P

MESH = pl.DeviceIdType.MESH
F32 = jnp.float32
BF16 = jnp.bfloat16
NZ = 16
NC = 16
KSTEP = 512
VMEM = 62 * 1024 * 1024

Z_PRIOR, Z_NEAR, Z_CPL, Z_Q, Z_ANS, Z_CPL2, Z_FOURTH = 0, 1, 2, 3, 5, 6, 7
C_ANS, C_U, C_UALL, C_OUT = 0, 2, 3, 4
K_PRIOR, K_INV, K_OUT, K_U = 0, 2, 3, 5


def split(x):
    hi = x.astype(BF16)
    return hi, (x - hi.astype(F32)).astype(BF16)


def dot3(a, b):
    (ah, al), (bh, bl) = a, b
    dot = functools.partial(jnp.dot, preferred_element_type=F32)
    return dot(ah, bh) + (dot(ah, bl) + dot(al, bh))


def tile(i, size):
    return pl.ds(i * size if isinstance(i, int) else pl.multiple_of(i * size, size), size)


FAR_Z = (8, 7, 9, 6, 10, 5, 11, 4, 12, 3, 13, 2, 14, 1, 15)
FAR_C = (10, 9, 11, 6, 14, 5, 7, 13, 15, 8, 2, 1, 3, 4, 12)


def place(z):
    return lax.rem(z, 4) * 4 + z // 4


def kernel(
    s_hbm, u_hbm, rs_hbm, d_hbm, c_hbm, o_ref,
    d_buf, c_buf, a_buf, s_buf, x_buf, pt, cx, p2, rb, ra, pm, rf, rsb, rst, wh, wl, qa, cg, pu, ru, ug, ubh, ubl, pp, rc, ga, xb, xs, ob,
    load_sem, zs, zr, cs, cr, ks, kr,
):
    row = lax.axis_index("row")
    c = lax.axis_index("col")
    z, k = row // 2, lax.rem(row, 2)
    ok = 1 - k

    def z_dev(i):
        return (lax.rem(z + i, NZ) * 2 + k, c)

    def c_at(i):
        return lax.rem(c // 4 + i // 4, 4) * 4 + lax.rem(c + i, 4)

    def c_dev(i):
        return (row, c_at(i))

    sibling = (z * 2 + ok, c)

    barrier = pltpu.get_barrier_semaphore()
    pl.semaphore_signal(barrier, inc=1, device_id=sibling, device_id_type=MESH)

    for i, j in zip(FAR_Z, FAR_C):
        pl.semaphore_signal(barrier, inc=1, device_id=z_dev(i), device_id_type=MESH)
        pl.semaphore_signal(barrier, inc=1, device_id=c_dev(j), device_id_type=MESH)

    def remote(src, dst, ssem, rsem, dev):
        return pltpu.make_async_remote_copy(
            src_ref=src, dst_ref=dst, send_sem=ssem, recv_sem=rsem, device_id=dev, device_id_type=MESH
        )

    def z_send(g, src, dst):
        for i in FAR_Z:
            remote(src(lax.rem(z + i, NZ)), dst(z), zs.at[g], zr.at[g], z_dev(i)).start()

    def z_all(g, ref):
        return remote(ref, ref, zs.at[g], zr.at[g], z_dev(1))

    def c_send(g, src, dst):
        for i in FAR_C:
            remote(src(c_at(i)), dst(c), cs.at[g], cr.at[g], c_dev(i)).start()

    def c_all(g, ref):
        return remote(ref, ref, cs.at[g], cr.at[g], c_dev(1))

    def block_sum(ref, size):
        parts = [ref[pl.ds(i * size, size)] for i in range(16)]
        while len(parts) > 1:
            parts = [one + two for one, two in zip(parts[::2], parts[1::2])]
        return parts[0]

    def k_copy(g, src, dst):
        return remote(src, dst, ks.at[g], kr.at[g], sibling)

    loads_a = [
        pltpu.make_async_copy(u_hbm.at[s, p], a_buf.at[pl.ds((p * 2 + s) * 64, 64)], load_sem.at[p * 2 + s])
        for p in range(2)
        for s in range(2)
    ]

    def load_s(s, j):
        return pltpu.make_async_copy(
            s_hbm.at[s, tile(j, KSTEP)], s_buf.at[s, tile(j, KSTEP)], load_sem.at[8 + s * 4 + j]
        )

    block = k * 2 + z // 8
    loads_r = [
        pltpu.make_async_copy(
            rs_hbm.at[s, p, :, tile(block, 128)], rsb.at[p, pl.ds(s * 64, 64)], load_sem.at[4 + p * 2 + s]
        )
        for p in range(2)
        for s in range(2)
    ]
    loads_r.append(pltpu.make_async_copy(d_hbm, d_buf.at[k], load_sem.at[16]))
    loads_r.append(pltpu.make_async_copy(c_hbm, c_buf, load_sem.at[17]))
    for copy in loads_a:
        copy.start()
    for j in range(1024 // KSTEP):
        load_s(0, j).start()
        load_s(1, j).start()
    for copy in loads_r:
        copy.start()

    for copy in loads_a:
        copy.wait()

    def prior_step(j, _):
        a = split(a_buf[:, tile(j, KSTEP)])
        for s in range(2):
            load_s(s, j).wait()
            part = dot3(a, split(s_buf[s, tile(j, KSTEP), :]))

            if j == 0:
                x_buf[s] = part
            else:
                x_buf[s] += part

    for j in range(1024 // KSTEP):
        prior_step(j, 0)
    for copy in loads_r:
        copy.wait()
    own_ct = cg.at[tile(place(z), 32)]
    own_ct[...] = jnp.concatenate([c_buf[0], -c_buf[1]], 1)

    def cpl_copy(i):
        return remote(own_ct, own_ct, zs.at[Z_CPL], zr.at[Z_CPL], z_dev(i))

    pl.semaphore_wait(barrier, 1 + (NZ - 1) + (NC - 1))
    for i in (8, 4, 12):
        cpl_copy(i).start()


    for p in range(2):
        lo, mid, hi = p * 128, p * 128 + 64, p * 128 + 128
        re = x_buf[0, lo:mid] + x_buf[1, mid:hi]
        im = x_buf[1, lo:mid] - x_buf[0, mid:hi]
        pt[p] = jnp.concatenate([re, im], axis=0).T
        rst[p] = rsb[p].T


    for p in range(2):
        k_copy(K_PRIOR + p, pt.at[p, tile(ok, 256)], cx.at[p]).start()
    own_d = d_buf.at[k]
    k_copy(K_INV, own_d, own_d).start()

    for p in range(2):
        k_copy(K_PRIOR + p, pt.at[p, tile(ok, 256)], cx.at[p]).wait_recv()
        if p == 0:
            p2[0] = pt[0, tile(k, 256)] + cx[0]
            z_send(Z_PRIOR, lambda i: p2.at[0, tile(i, 16)], lambda i: rb.at[tile(i, 16)])
    for i in range(NZ):
        p2[1, tile(place(i), 16)] = pt[1, pl.ds(pl.multiple_of(k * 256 + i * 16, 16), 16)] + cx[1, tile(i, 16)]

    near = ((0, 1, 0, 0, 64), (1, -1, 1, 0, 64), (2, 2, 2, 0, 32), (3, -2, 2, 32, 32))

    def near_copy(n, step, to, first, rows):
        group = lax.rem(z + step + NZ, 4)
        src = p2.at[1, pl.ds(pl.multiple_of(group * 64 + first, 32), rows)]
        return remote(src, ra.at[pl.ds(to * 64 + first, rows)], zs.at[Z_NEAR], zr.at[Z_NEAR], z_dev(step + NZ))

    def fourth_copy(i):
        src = pm.at[tile(lax.rem(z + i, NZ) // 4, 16)]
        return remote(src, rf.at[i // 4], zs.at[Z_FOURTH], zr.at[Z_FOURTH], z_dev(i))

    for args in near:
        near_copy(*args).start()
    k_copy(K_INV, own_d, d_buf.at[ok]).wait_recv()
    at = lax.broadcasted_iota(jnp.int32, (32, 64), 0) - lax.broadcasted_iota(jnp.int32, (32, 64), 1)
    for p in range(2):
        lines = []
        for q in range(2):
            low = c * 64 <= at + (z * 64 + q * 32)
            re, im = (jnp.where(low, d_buf[q, s, p], 0.0) for s in range(2))
            lines += [jnp.concatenate([re, -im], 1), jnp.concatenate([im, re], 1)]
        wh[p], wl[p] = split(jnp.concatenate(lines, 0).T)

    onward = ((0, 1, 0, 128), (1, -1, 0, 128), (2, 2, 0, 64), (3, -2, 64, 64))

    def onward_copy(n, step, first, rows, frm):
        ref = cg.at[pl.ds(pl.multiple_of(lax.rem(frm, 4) * 128 + first, 64), rows)]
        return remote(ref, ref, zs.at[Z_CPL2], zr.at[Z_CPL2], z_dev(step + NZ))

    z_all(Z_CPL, cg.at[pl.ds(0, 96)]).wait_recv()
    for n, step, first, rows in onward:
        onward_copy(n, step, first, rows, z).start()

    z_all(Z_NEAR, ra).wait_recv()
    pm[...] = p2[1, tile(lax.rem(z, 4), 64)] + ra[0:64] + (ra[64:128] + ra[128:192])
    for i in (8, 4, 12):
        fourth_copy(i).start()

    def gather_q(p):
        if p == 0:
            rb[tile(z, 16)] = p2[0, tile(z, 16)]
            z_all(Z_PRIOR, rb.at[pl.ds(0, 240)]).wait_recv()
            total = block_sum(rb, 16)
        else:
            z_all(Z_FOURTH, rf.at[pl.ds(1, 3)]).wait_recv()
            total = pm[tile(z // 4, 16)] + rf[1] + (rf[2] + rf[3])
        own_q = qa.at[p, tile(z, 16)]
        own_q[...] = rst[p, tile(lax.rem(z, 8), 16)] - total
        z_send(Z_Q + p, lambda i: own_q, lambda i: qa.at[p, tile(i, 16)])

    gather_q(0)

    z_all(Z_CPL2, cg.at[pl.ds(0, 384)]).wait_recv()
    pu[...] = dot3(split(cg[...]), (wh[1], wl[1]))
    c_send(C_U, lambda i: pu.at[tile(i, 32)], lambda i: ru.at[tile(i, 32)])
    gather_q(1)

    def lower(p):
        z_all(Z_Q + p, qa.at[p, pl.ds(0, 240)]).wait_recv()
        pp[p] = dot3(split(qa[p]), (wh[p], wl[p]))
        c_send(C_ANS + p, lambda i: pp.at[p, tile(i, 16)], lambda i: rc.at[p, tile(i, 16)])

    def summed(p):
        rc[p, tile(c, 16)] = pp[p, tile(c, 16)]
        c_all(C_ANS + p, rc.at[p, pl.ds(0, 240)]).wait_recv()
        return block_sum(rc.at[p], 16)

    lane = lax.broadcasted_iota(jnp.int32, (16, 128), 1)
    own_lanes = lane // 64 == k

    def swap(p):
        return k_copy(K_OUT + p, xb.at[p], xs.at[p])

    def share(p):
        swap(p).wait_recv()
        own = ob.at[p, tile(c, 16)]
        own[...] = jnp.where(own_lanes, xb[p], pltpu.roll(xs[p], 64, 1))
        c_send(C_OUT + p, lambda i: own, lambda i: ob.at[p, tile(i, 16)])

    lower(0)

    ru[tile(c, 32)] = pu[tile(c, 32)]
    c_all(C_U, ru.at[pl.ds(0, 480)]).wait_recv()
    own_u = ug.at[k, tile(c, 32)]
    own_u[...] = block_sum(ru, 32)
    c_send(C_UALL, lambda i: own_u, lambda i: ug.at[k, tile(i, 32)])

    own_a = ga.at[:, tile(z, 128)]
    answer_0 = summed(0)
    own_a[...] = answer_0
    z_send(Z_ANS, lambda i: own_a, lambda i: ga.at[:, tile(i, 128)])
    xb[0] = answer_0
    swap(0).start()

    lower(1)

    c_all(C_UALL, ug.at[k, pl.ds(0, 480)]).wait_recv()
    half = ug.at[k]
    k_copy(K_U, half, half).start()
    share(0)

    k_copy(K_U, half, ug.at[ok]).wait_recv()
    imag = lax.rem(lax.broadcasted_iota(jnp.int32, (32, 128), 1) // 32, 2) == 1

    def weigh(i, _):
        for q in range(2):
            v = ug[q, tile(i, 32)]
            v2 = jnp.where(imag, pltpu.roll(v, 32, 1), -pltpu.roll(v, 96, 1))
            hi, lo = split(jnp.concatenate([v, v2], axis=0))
            ubh[tile(place(i) * 2 + q, 64)] = hi
            ubl[tile(place(i) * 2 + q, 64)] = lo
        return 0

    lax.fori_loop(0, NC, weigh, 0)
    own_1 = summed(1)

    z_all(Z_ANS, ga.at[:, pl.ds(0, 15 * 128)]).wait_recv()
    xb[1] = own_1 - dot3(split(ga[...]), (ubh[...], ubl[...]))
    swap(1).start()
    share(1)

    for p in range(2):
        c_all(C_OUT + p, ob.at[p, pl.ds(0, 240)]).wait_recv()
        turned = ob[p].T
        for h in range(2):
            for s in range(2):
                at = (h * 2 + s) * 32
                o_ref[s, p, :, pl.ds(h * 256, 256)] = turned[at : at + 32]

    z_all(Z_PRIOR, rb.at[pl.ds(0, 240)]).wait_send()
    z_all(Z_NEAR, ra).wait_send()
    z_all(Z_CPL, cg.at[pl.ds(0, 96)]).wait_send()
    z_all(Z_CPL2, cg.at[pl.ds(0, 384)]).wait_send()
    z_all(Z_FOURTH, rf.at[pl.ds(1, 3)]).wait_send()
    z_all(Z_ANS, ga.at[:, pl.ds(0, 15 * 128)]).wait_send()
    c_all(C_U, ru.at[pl.ds(0, 480)]).wait_send()
    c_all(C_UALL, ug.at[k, pl.ds(0, 480)]).wait_send()
    for p in range(2):
        z_all(Z_Q + p, qa.at[p, pl.ds(0, 240)]).wait_send()
        c_all(C_ANS + p, rc.at[p, pl.ds(0, 240)]).wait_send()
        c_all(C_OUT + p, ob.at[p, pl.ds(0, 240)]).wait_send()
    k_copy(0, cx.at[0], cx.at[0]).wait_send()
    k_copy(1, cx.at[1], cx.at[1]).wait_send()
    k_copy(K_INV, own_d, own_d).wait_send()
    k_copy(K_U, half, half).wait_send()
    for p in range(2):
        swap(p).wait_send()


def per_device(solved, upper_cols, coupling, inverse_diag, right_side):
    vmem = pl.BlockSpec(memory_space=pltpu.VMEM)
    hbm = pl.BlockSpec(memory_space=pltpu.HBM)
    f = lambda *shape: pltpu.VMEM(shape, F32)
    b = lambda *shape: pltpu.VMEM(shape, BF16)
    return pl.pallas_call(
        kernel,
        out_shape=pltpu.VMEM((2, 2, 32, 512), F32),
        in_specs=[hbm] * 5,
        out_specs=vmem,
        scratch_shapes=[
            f(2, 2, 2, 32, 64), f(2, 32, 64), f(256, 1024), f(2, 1024, 512), f(2, 256, 512), f(2, 512, 128),
            f(2, 256, 128), f(2, 256, 128), f(256, 128), f(192, 128), f(64, 128), f(4, 16, 128), f(2, 128, 128), f(2, 128, 128),
            b(2, 128, 128), b(2, 128, 128), f(2, 256, 128), f(512, 128), f(512, 128), f(512, 128), f(2, 512, 128),
            b(2048, 128), b(2048, 128), f(2, 256, 128), f(2, 256, 128), f(16, 2048), f(2, 16, 128), f(2, 16, 128),
            f(2, 256, 128),
            pltpu.SemaphoreType.DMA((18,)),
            pltpu.SemaphoreType.DMA((8,)), pltpu.SemaphoreType.DMA((8,)),
            pltpu.SemaphoreType.DMA((6,)), pltpu.SemaphoreType.DMA((6,)),
            pltpu.SemaphoreType.DMA((6,)), pltpu.SemaphoreType.DMA((6,)),
        ],
        compiler_params=pltpu.CompilerParams(
            collective_id=0, has_side_effects=True, vmem_limit_bytes=VMEM
        ),
        name="panels",
    )(solved, upper_cols, right_side, inverse_diag, jnp.swapaxes(coupling, 1, 2))


def solution(mesh):
    in_specs = (
        P(None, "row", None),
        P(None, None, "col", "row"),
        P(None, "col", "row"),
        P(None, None, "row", "col"),
        P(None, None, "col", None),
    )
    out_specs = P(None, None, "row", None)
    return jax.shard_map(
        per_device, mesh=mesh, in_specs=in_specs, out_specs=out_specs, check_vma=False
    )
```

```python
import functools

import jax
import jax.numpy as jnp
from jax import lax
from jax.experimental import pallas as pl
from jax.experimental.pallas import tpu as pltpu
from jax.sharding import PartitionSpec as P

MESH = pl.DeviceIdType.MESH
F32 = jnp.float32
BF16 = jnp.bfloat16
NZ = 16
NC = 16
KSTEP = 512
VMEM = 62 * 1024 * 1024

Z_PRIOR, Z_NEAR, Z_CPL, Z_Q, Z_ANS, Z_CPL2, Z_FOURTH = 0, 1, 2, 3, 5, 6, 7
C_ANS, C_U, C_UALL, C_OUT = 0, 2, 3, 4
K_PRIOR, K_INV, K_OUT, K_U = 0, 2, 3, 5


def split(x):
    hi = x.astype(BF16)
    return hi, (x - hi.astype(F32)).astype(BF16)


def dot3(a, b):
    (ah, al), (bh, bl) = a, b
    dot = functools.partial(jnp.dot, preferred_element_type=F32)
    return dot(ah, bh) + (dot(ah, bl) + dot(al, bh))


def tile(i, size):
    return pl.ds(i * size if isinstance(i, int) else pl.multiple_of(i * size, size), size)


FAR_Z = (8, 7, 9, 6, 10, 5, 11, 4, 12, 3, 13, 2, 14, 1, 15)
FAR_C = (10, 9, 11, 6, 14, 5, 7, 13, 15, 8, 2, 1, 3, 4, 12)


def place(z):
    return lax.rem(z, 4) * 4 + z // 4


def kernel(
    s_hbm, u_hbm, rs_hbm, d_hbm, c_hbm, o_ref,
    d_buf, c_buf, a_buf, s_buf, x_buf, pt, cx, p2, rb, ra, pm, rf, rsb, rst, wh, wl, qa, cg, pu, ru, ug, ubh, ubl, pp, rc, ga, xb, xs, ob,
    load_sem, zs, zr, cs, cr, ks, kr,
):
    row = lax.axis_index("row")
    c = lax.axis_index("col")
    z, k = row // 2, lax.rem(row, 2)
    ok = 1 - k

    def z_dev(i):
        return (lax.rem(z + i, NZ) * 2 + k, c)

    def c_at(i):
        return lax.rem(c // 4 + i // 4, 4) * 4 + lax.rem(c + i, 4)

    def c_dev(i):
        return (row, c_at(i))

    sibling = (z * 2 + ok, c)

    barrier = pltpu.get_barrier_semaphore()
    pl.semaphore_signal(barrier, inc=1, device_id=sibling, device_id_type=MESH)

    for i, j in zip(FAR_Z, FAR_C):
        pl.semaphore_signal(barrier, inc=1, device_id=z_dev(i), device_id_type=MESH)
        pl.semaphore_signal(barrier, inc=1, device_id=c_dev(j), device_id_type=MESH)

    def remote(src, dst, ssem, rsem, dev):
        return pltpu.make_async_remote_copy(
            src_ref=src, dst_ref=dst, send_sem=ssem, recv_sem=rsem, device_id=dev, device_id_type=MESH
        )

    def z_send(g, src, dst):
        for i in FAR_Z:
            remote(src(lax.rem(z + i, NZ)), dst(z), zs.at[g], zr.at[g], z_dev(i)).start()

    def z_all(g, ref):
        return remote(ref, ref, zs.at[g], zr.at[g], z_dev(1))

    def c_send(g, src, dst):
        for i in FAR_C:
            remote(src(c_at(i)), dst(c), cs.at[g], cr.at[g], c_dev(i)).start()

    def c_all(g, ref):
        return remote(ref, ref, cs.at[g], cr.at[g], c_dev(1))

    def block_sum(ref, size):
        parts = [ref[pl.ds(i * size, size)] for i in range(16)]
        while len(parts) > 1:
            parts = [one + two for one, two in zip(parts[::2], parts[1::2])]
        return parts[0]

    def k_copy(g, src, dst):
        return remote(src, dst, ks.at[g], kr.at[g], sibling)

    loads_a = [
        pltpu.make_async_copy(u_hbm.at[s, p], a_buf.at[pl.ds((p * 2 + s) * 64, 64)], load_sem.at[p * 2 + s])
        for p in range(2)
        for s in range(2)
    ]

    def load_s(s, j):
        return pltpu.make_async_copy(
            s_hbm.at[s, tile(j, KSTEP)], s_buf.at[s, tile(j, KSTEP)], load_sem.at[8 + s * 4 + j]
        )

    block = k * 2 + z // 8
    loads_r = [
        pltpu.make_async_copy(
            rs_hbm.at[s, p, :, tile(block, 128)], rsb.at[p, pl.ds(s * 64, 64)], load_sem.at[4 + p * 2 + s]
        )
        for p in range(2)
        for s in range(2)
    ]
    loads_r.append(pltpu.make_async_copy(d_hbm, d_buf.at[k], load_sem.at[16]))
    loads_r.append(pltpu.make_async_copy(c_hbm, c_buf, load_sem.at[17]))
    for copy in loads_a:
        copy.start()
    for j in range(1024 // KSTEP):
        load_s(0, j).start()
        load_s(1, j).start()
    for copy in loads_r:
        copy.start()

    for copy in loads_a:
        copy.wait()

    def prior_step(j, _):
        a = split(a_buf[:, tile(j, KSTEP)])
        for s in range(2):
            load_s(s, j).wait()
            part = dot3(a, split(s_buf[s, tile(j, KSTEP), :]))

            if j == 0:
                x_buf[s] = part
            else:
                x_buf[s] += part

    for j in range(1024 // KSTEP):
        prior_step(j, 0)
    for copy in loads_r:
        copy.wait()
    own_ct = cg.at[tile(place(z), 32)]
    own_ct[...] = jnp.concatenate([c_buf[0], -c_buf[1]], 1)

    def cpl_copy(i):
        return remote(own_ct, own_ct, zs.at[Z_CPL], zr.at[Z_CPL], z_dev(i))


    for p in range(2):
        lo, mid, hi = p * 128, p * 128 + 64, p * 128 + 128
        re = x_buf[0, lo:mid] + x_buf[1, mid:hi]
        im = x_buf[1, lo:mid] - x_buf[0, mid:hi]
        pt[p] = jnp.concatenate([re, im], axis=0).T
        rst[p] = rsb[p].T


    pl.semaphore_wait(barrier, 1 + (NZ - 1) + (NC - 1))
    for i in (8, 4, 12):
        cpl_copy(i).start()
    for p in range(2):
        k_copy(K_PRIOR + p, pt.at[p, tile(ok, 256)], cx.at[p]).start()
    own_d = d_buf.at[k]
    k_copy(K_INV, own_d, own_d).start()

    for p in range(2):
        k_copy(K_PRIOR + p, pt.at[p, tile(ok, 256)], cx.at[p]).wait_recv()
        if p == 0:
            p2[0] = pt[0, tile(k, 256)] + cx[0]
    for i in range(NZ):
        p2[1, tile(place(i), 16)] = pt[1, pl.ds(pl.multiple_of(k * 256 + i * 16, 16), 16)] + cx[1, tile(i, 16)]

    near = ((0, 1, 0, 0, 64), (1, -1, 1, 0, 64), (2, 2, 2, 0, 32), (3, -2, 2, 32, 32))

    def near_copy(n, step, to, first, rows):
        group = lax.rem(z + step + NZ, 4)
        src = p2.at[1, pl.ds(pl.multiple_of(group * 64 + first, 32), rows)]
        return remote(src, ra.at[pl.ds(to * 64 + first, rows)], zs.at[Z_NEAR], zr.at[Z_NEAR], z_dev(step + NZ))

    def fourth_copy(i):
        src = pm.at[tile(lax.rem(z + i, NZ) // 4, 16)]
        return remote(src, rf.at[i // 4], zs.at[Z_FOURTH], zr.at[Z_FOURTH], z_dev(i))

    for args in near:
        near_copy(*args).start()
    z_send(Z_PRIOR, lambda i: p2.at[0, tile(i, 16)], lambda i: rb.at[tile(i, 16)])
    k_copy(K_INV, own_d, d_buf.at[ok]).wait_recv()
    at = lax.broadcasted_iota(jnp.int32, (32, 64), 0) - lax.broadcasted_iota(jnp.int32, (32, 64), 1)
    for p in range(2):
        lines = []
        for q in range(2):
            low = c * 64 <= at + (z * 64 + q * 32)
            re, im = (jnp.where(low, d_buf[q, s, p], 0.0) for s in range(2))
            lines += [jnp.concatenate([re, -im], 1), jnp.concatenate([im, re], 1)]
        wh[p], wl[p] = split(jnp.concatenate(lines, 0).T)

    onward = ((0, 1, 0, 128), (1, -1, 0, 128), (2, 2, 0, 64), (3, -2, 64, 64))

    def onward_copy(n, step, first, rows, frm):
        ref = cg.at[pl.ds(pl.multiple_of(lax.rem(frm, 4) * 128 + first, 64), rows)]
        return remote(ref, ref, zs.at[Z_CPL2], zr.at[Z_CPL2], z_dev(step + NZ))

    z_all(Z_CPL, cg.at[pl.ds(0, 96)]).wait_recv()
    for n, step, first, rows in onward:
        onward_copy(n, step, first, rows, z).start()

    z_all(Z_NEAR, ra).wait_recv()
    pm[...] = p2[1, tile(lax.rem(z, 4), 64)] + ra[0:64] + (ra[64:128] + ra[128:192])
    for i in (8, 4, 12):
        fourth_copy(i).start()

    def gather_q(p):
        if p == 0:
            rb[tile(z, 16)] = p2[0, tile(z, 16)]
            z_all(Z_PRIOR, rb.at[pl.ds(0, 240)]).wait_recv()
            total = block_sum(rb, 16)
        else:
            z_all(Z_FOURTH, rf.at[pl.ds(1, 3)]).wait_recv()
            total = pm[tile(z // 4, 16)] + rf[1] + (rf[2] + rf[3])
        own_q = qa.at[p, tile(z, 16)]
        own_q[...] = rst[p, tile(lax.rem(z, 8), 16)] - total
        z_send(Z_Q + p, lambda i: own_q, lambda i: qa.at[p, tile(i, 16)])

    gather_q(0)

    z_all(Z_CPL2, cg.at[pl.ds(0, 384)]).wait_recv()
    pu[...] = dot3(split(cg[...]), (wh[1], wl[1]))
    c_send(C_U, lambda i: pu.at[tile(i, 32)], lambda i: ru.at[tile(i, 32)])
    gather_q(1)

    def lower(p):
        z_all(Z_Q + p, qa.at[p, pl.ds(0, 240)]).wait_recv()
        pp[p] = dot3(split(qa[p]), (wh[p], wl[p]))
        c_send(C_ANS + p, lambda i: pp.at[p, tile(i, 16)], lambda i: rc.at[p, tile(i, 16)])

    def summed(p):
        rc[p, tile(c, 16)] = pp[p, tile(c, 16)]
        c_all(C_ANS + p, rc.at[p, pl.ds(0, 240)]).wait_recv()
        return block_sum(rc.at[p], 16)

    lane = lax.broadcasted_iota(jnp.int32, (16, 128), 1)
    own_lanes = lane // 64 == k

    def swap(p):
        return k_copy(K_OUT + p, xb.at[p], xs.at[p])

    def share(p):
        swap(p).wait_recv()
        own = ob.at[p, tile(c, 16)]
        own[...] = jnp.where(own_lanes, xb[p], pltpu.roll(xs[p], 64, 1))
        c_send(C_OUT + p, lambda i: own, lambda i: ob.at[p, tile(i, 16)])

    lower(0)

    ru[tile(c, 32)] = pu[tile(c, 32)]
    c_all(C_U, ru.at[pl.ds(0, 480)]).wait_recv()
    own_u = ug.at[k, tile(c, 32)]
    own_u[...] = block_sum(ru, 32)
    c_send(C_UALL, lambda i: own_u, lambda i: ug.at[k, tile(i, 32)])

    own_a = ga.at[:, tile(z, 128)]
    answer_0 = summed(0)
    own_a[...] = answer_0
    z_send(Z_ANS, lambda i: own_a, lambda i: ga.at[:, tile(i, 128)])
    xb[0] = answer_0
    swap(0).start()

    c_all(C_UALL, ug.at[k, pl.ds(0, 480)]).wait_recv()
    half = ug.at[k]
    k_copy(K_U, half, half).start()
    lower(1)

    share(0)

    k_copy(K_U, half, ug.at[ok]).wait_recv()
    imag = lax.rem(lax.broadcasted_iota(jnp.int32, (32, 128), 1) // 32, 2) == 1

    def weigh(i, _):
        for q in range(2):
            v = ug[q, tile(i, 32)]
            v2 = jnp.where(imag, pltpu.roll(v, 32, 1), -pltpu.roll(v, 96, 1))
            hi, lo = split(jnp.concatenate([v, v2], axis=0))
            ubh[tile(place(i) * 2 + q, 64)] = hi
            ubl[tile(place(i) * 2 + q, 64)] = lo
        return 0

    lax.fori_loop(0, NC, weigh, 0)
    own_1 = summed(1)

    z_all(Z_ANS, ga.at[:, pl.ds(0, 15 * 128)]).wait_recv()
    xb[1] = own_1 - dot3(split(ga[...]), (ubh[...], ubl[...]))
    swap(1).start()
    share(1)

    for p in range(2):
        c_all(C_OUT + p, ob.at[p, pl.ds(0, 240)]).wait_recv()
        turned = ob[p].T
        for h in range(2):
            for s in range(2):
                at = (h * 2 + s) * 32
                o_ref[s, p, :, pl.ds(h * 256, 256)] = turned[at : at + 32]

    z_all(Z_PRIOR, rb.at[pl.ds(0, 240)]).wait_send()
    z_all(Z_NEAR, ra).wait_send()
    z_all(Z_CPL, cg.at[pl.ds(0, 96)]).wait_send()
    z_all(Z_CPL2, cg.at[pl.ds(0, 384)]).wait_send()
    z_all(Z_FOURTH, rf.at[pl.ds(1, 3)]).wait_send()
    z_all(Z_ANS, ga.at[:, pl.ds(0, 15 * 128)]).wait_send()
    c_all(C_U, ru.at[pl.ds(0, 480)]).wait_send()
    c_all(C_UALL, ug.at[k, pl.ds(0, 480)]).wait_send()
    for p in range(2):
        z_all(Z_Q + p, qa.at[p, pl.ds(0, 240)]).wait_send()
        c_all(C_ANS + p, rc.at[p, pl.ds(0, 240)]).wait_send()
        c_all(C_OUT + p, ob.at[p, pl.ds(0, 240)]).wait_send()
    k_copy(0, cx.at[0], cx.at[0]).wait_send()
    k_copy(1, cx.at[1], cx.at[1]).wait_send()
    k_copy(K_INV, own_d, own_d).wait_send()
    k_copy(K_U, half, half).wait_send()
    for p in range(2):
        swap(p).wait_send()


def per_device(solved, upper_cols, coupling, inverse_diag, right_side):
    vmem = pl.BlockSpec(memory_space=pltpu.VMEM)
    hbm = pl.BlockSpec(memory_space=pltpu.HBM)
    f = lambda *shape: pltpu.VMEM(shape, F32)
    b = lambda *shape: pltpu.VMEM(shape, BF16)
    return pl.pallas_call(
        kernel,
        out_shape=pltpu.VMEM((2, 2, 32, 512), F32),
        in_specs=[hbm] * 5,
        out_specs=vmem,
        scratch_shapes=[
            f(2, 2, 2, 32, 64), f(2, 32, 64), f(256, 1024), f(2, 1024, 512), f(2, 256, 512), f(2, 512, 128),
            f(2, 256, 128), f(2, 256, 128), f(256, 128), f(192, 128), f(64, 128), f(4, 16, 128), f(2, 128, 128), f(2, 128, 128),
            b(2, 128, 128), b(2, 128, 128), f(2, 256, 128), f(512, 128), f(512, 128), f(512, 128), f(2, 512, 128),
            b(2048, 128), b(2048, 128), f(2, 256, 128), f(2, 256, 128), f(16, 2048), f(2, 16, 128), f(2, 16, 128),
            f(2, 256, 128),
            pltpu.SemaphoreType.DMA((18,)),
            pltpu.SemaphoreType.DMA((8,)), pltpu.SemaphoreType.DMA((8,)),
            pltpu.SemaphoreType.DMA((6,)), pltpu.SemaphoreType.DMA((6,)),
            pltpu.SemaphoreType.DMA((6,)), pltpu.SemaphoreType.DMA((6,)),
        ],
        compiler_params=pltpu.CompilerParams(
            collective_id=0, has_side_effects=True, vmem_limit_bytes=VMEM
        ),
        name="panels",
    )(solved, upper_cols, right_side, inverse_diag, jnp.swapaxes(coupling, 1, 2))


def solution(mesh):
    in_specs = (
        P(None, "row", None),
        P(None, None, "col", "row"),
        P(None, "col", "row"),
        P(None, None, "row", "col"),
        P(None, None, "col", None),
    )
    out_specs = P(None, None, "row", None)
    return jax.shard_map(
        per_device, mesh=mesh, in_specs=in_specs, out_specs=out_specs, check_vma=False
    )
```

```python
import functools

import jax
import jax.numpy as jnp
from jax import lax
from jax.experimental import pallas as pl
from jax.experimental.pallas import tpu as pltpu
from jax.sharding import PartitionSpec as P

MESH = pl.DeviceIdType.MESH
F32 = jnp.float32
BF16 = jnp.bfloat16
NZ = 16
NC = 16
KSTEP = 512
VMEM = 62 * 1024 * 1024

Z_PRIOR, Z_NEAR, Z_CPL, Z_Q, Z_ANS, Z_CPL2, Z_FOURTH = 0, 1, 2, 3, 5, 6, 7
C_ANS, C_U, C_UALL, C_OUT = 0, 2, 3, 4
K_PRIOR, K_INV, K_OUT, K_U = 0, 2, 3, 5


def split(x):
    hi = x.astype(BF16)
    return hi, (x - hi.astype(F32)).astype(BF16)


def dot3(a, b):
    (ah, al), (bh, bl) = a, b
    dot = functools.partial(jnp.dot, preferred_element_type=F32)
    return dot(ah, bh) + (dot(ah, bl) + dot(al, bh))


def tile(i, size):
    return pl.ds(i * size if isinstance(i, int) else pl.multiple_of(i * size, size), size)


FAR_Z = (8, 7, 9, 6, 10, 5, 11, 4, 12, 3, 13, 2, 14, 1, 15)
FAR_C = (10, 9, 11, 6, 14, 5, 7, 13, 15, 8, 2, 1, 3, 4, 12)


def place(z):
    return lax.rem(z, 4) * 4 + z // 4


def kernel(
    s_hbm, u_hbm, rs_hbm, d_hbm, c_hbm, o_ref,
    d_buf, c_buf, a_buf, s_buf, x_buf, pt, cx, p2, rb, ra, pm, rf, rsb, rst, wh, wl, qa, cg, pu, ru, ug, ubh, ubl, pp, rc, ga, xb, xs, ob,
    load_sem, zs, zr, cs, cr, ks, kr,
):
    row = lax.axis_index("row")
    c = lax.axis_index("col")
    z, k = row // 2, lax.rem(row, 2)
    ok = 1 - k

    def z_dev(i):
        return (lax.rem(z + i, NZ) * 2 + k, c)

    def c_at(i):
        return lax.rem(c // 4 + i // 4, 4) * 4 + lax.rem(c + i, 4)

    def c_dev(i):
        return (row, c_at(i))

    sibling = (z * 2 + ok, c)

    barrier = pltpu.get_barrier_semaphore()
    pl.semaphore_signal(barrier, inc=1, device_id=sibling, device_id_type=MESH)

    for i, j in zip(FAR_Z, FAR_C):
        pl.semaphore_signal(barrier, inc=1, device_id=z_dev(i), device_id_type=MESH)
        pl.semaphore_signal(barrier, inc=1, device_id=c_dev(j), device_id_type=MESH)

    def remote(src, dst, ssem, rsem, dev):
        return pltpu.make_async_remote_copy(
            src_ref=src, dst_ref=dst, send_sem=ssem, recv_sem=rsem, device_id=dev, device_id_type=MESH
        )

    def z_send(g, src, dst):
        for i in FAR_Z:
            remote(src(lax.rem(z + i, NZ)), dst(z), zs.at[g], zr.at[g], z_dev(i)).start()

    def z_all(g, ref):
        return remote(ref, ref, zs.at[g], zr.at[g], z_dev(1))

    def c_send(g, src, dst):
        for i in FAR_C:
            remote(src(c_at(i)), dst(c), cs.at[g], cr.at[g], c_dev(i)).start()

    def c_all(g, ref):
        return remote(ref, ref, cs.at[g], cr.at[g], c_dev(1))

    def block_sum(ref, size):
        parts = [ref[pl.ds(i * size, size)] for i in range(16)]
        while len(parts) > 1:
            parts = [one + two for one, two in zip(parts[::2], parts[1::2])]
        return parts[0]

    def k_copy(g, src, dst):
        return remote(src, dst, ks.at[g], kr.at[g], sibling)

    loads_a = [
        pltpu.make_async_copy(u_hbm.at[s, p], a_buf.at[pl.ds((p * 2 + s) * 64, 64)], load_sem.at[p * 2 + s])
        for p in range(2)
        for s in range(2)
    ]

    def load_s(s, j):
        return pltpu.make_async_copy(
            s_hbm.at[s, tile(j, KSTEP)], s_buf.at[s, tile(j, KSTEP)], load_sem.at[8 + s * 4 + j]
        )

    block = k * 2 + z // 8
    loads_r = [
        pltpu.make_async_copy(
            rs_hbm.at[s, p, :, tile(block, 128)], rsb.at[p, pl.ds(s * 64, 64)], load_sem.at[4 + p * 2 + s]
        )
        for p in range(2)
        for s in range(2)
    ]
    loads_r.append(pltpu.make_async_copy(d_hbm, d_buf.at[k], load_sem.at[16]))
    loads_r.append(pltpu.make_async_copy(c_hbm, c_buf, load_sem.at[17]))
    for copy in loads_a:
        copy.start()
    for j in range(1024 // KSTEP):
        load_s(0, j).start()
        load_s(1, j).start()
    for copy in loads_r:
        copy.start()

    for copy in loads_a:
        copy.wait()

    def prior_step(j, _):
        a = split(a_buf[:, tile(j, KSTEP)])
        for s in range(2):
            load_s(s, j).wait()
            part = dot3(a, split(s_buf[s, tile(j, KSTEP), :]))

            if j == 0:
                x_buf[s] = part
            else:
                x_buf[s] += part

    for j in range(1024 // KSTEP):
        prior_step(j, 0)
    for copy in loads_r:
        copy.wait()
    own_ct = cg.at[tile(place(z), 32)]
    own_ct[...] = jnp.concatenate([c_buf[0], -c_buf[1]], 1)

    def cpl_copy(i):
        return remote(own_ct, own_ct, zs.at[Z_CPL], zr.at[Z_CPL], z_dev(i))


    for p in range(2):
        lo, mid, hi = p * 128, p * 128 + 64, p * 128 + 128
        re = x_buf[0, lo:mid] + x_buf[1, mid:hi]
        im = x_buf[1, lo:mid] - x_buf[0, mid:hi]
        pt[p] = jnp.concatenate([re, im], axis=0).T
        rst[p] = rsb[p].T


    pl.semaphore_wait(barrier, 1 + (NZ - 1) + (NC - 1))
    for i in (8, 4, 12):
        cpl_copy(i).start()
    for p in range(2):
        k_copy(K_PRIOR + p, pt.at[p, tile(ok, 256)], cx.at[p]).start()
    own_d = d_buf.at[k]
    k_copy(K_INV, own_d, own_d).start()

    for p in range(2):
        k_copy(K_PRIOR + p, pt.at[p, tile(ok, 256)], cx.at[p]).wait_recv()
        if p == 0:
            p2[0] = pt[0, tile(k, 256)] + cx[0]
    for i in range(NZ):
        p2[1, tile(place(i), 16)] = pt[1, pl.ds(pl.multiple_of(k * 256 + i * 16, 16), 16)] + cx[1, tile(i, 16)]

    near = ((0, 1, 0, 0, 64), (1, -1, 1, 0, 64), (2, 2, 2, 0, 32), (3, -2, 2, 32, 32))

    def near_copy(n, step, to, first, rows):
        group = lax.rem(z + step + NZ, 4)
        src = p2.at[1, pl.ds(pl.multiple_of(group * 64 + first, 32), rows)]
        return remote(src, ra.at[pl.ds(to * 64 + first, rows)], zs.at[Z_NEAR], zr.at[Z_NEAR], z_dev(step + NZ))

    def fourth_copy(i):
        src = pm.at[tile(lax.rem(z + i, NZ) // 4, 16)]
        return remote(src, rf.at[i // 4], zs.at[Z_FOURTH], zr.at[Z_FOURTH], z_dev(i))

    for args in near:
        near_copy(*args).start()
    z_send(Z_PRIOR, lambda i: p2.at[0, tile(i, 16)], lambda i: rb.at[tile(i, 16)])
    k_copy(K_INV, own_d, d_buf.at[ok]).wait_recv()
    at = lax.broadcasted_iota(jnp.int32, (32, 64), 0) - lax.broadcasted_iota(jnp.int32, (32, 64), 1)
    for p in range(2):
        lines = []
        for q in range(2):
            low = c * 64 <= at + (z * 64 + q * 32)
            re, im = (jnp.where(low, d_buf[q, s, p], 0.0) for s in range(2))
            lines += [jnp.concatenate([re, -im], 1), jnp.concatenate([im, re], 1)]
        wh[p], wl[p] = split(jnp.concatenate(lines, 0).T)

    onward = ((0, 1, 0, 128), (1, -1, 0, 128), (2, 2, 0, 64), (3, -2, 64, 64))

    def onward_copy(n, step, first, rows, frm):
        ref = cg.at[pl.ds(pl.multiple_of(lax.rem(frm, 4) * 128 + first, 64), rows)]
        return remote(ref, ref, zs.at[Z_CPL2], zr.at[Z_CPL2], z_dev(step + NZ))

    z_all(Z_CPL, cg.at[pl.ds(0, 96)]).wait_recv()
    for n, step, first, rows in onward:
        onward_copy(n, step, first, rows, z).start()

    z_all(Z_NEAR, ra).wait_recv()
    pm[...] = p2[1, tile(lax.rem(z, 4), 64)] + ra[0:64] + (ra[64:128] + ra[128:192])
    for i in (8, 4, 12):
        fourth_copy(i).start()

    def gather_q(p):
        if p == 0:
            rb[tile(z, 16)] = p2[0, tile(z, 16)]
            z_all(Z_PRIOR, rb.at[pl.ds(0, 240)]).wait_recv()
            total = block_sum(rb, 16)
        else:
            z_all(Z_FOURTH, rf.at[pl.ds(1, 3)]).wait_recv()
            total = pm[tile(z // 4, 16)] + rf[1] + (rf[2] + rf[3])
        own_q = qa.at[p, tile(z, 16)]
        own_q[...] = rst[p, tile(lax.rem(z, 8), 16)] - total
        z_send(Z_Q + p, lambda i: own_q, lambda i: qa.at[p, tile(i, 16)])

    gather_q(0)

    z_all(Z_CPL2, cg.at[pl.ds(0, 384)]).wait_recv()
    pu[...] = dot3(split(cg[...]), (wh[1], wl[1]))
    c_send(C_U, lambda i: pu.at[tile(i, 32)], lambda i: ru.at[tile(i, 32)])
    gather_q(1)

    def lower(p):
        z_all(Z_Q + p, qa.at[p, pl.ds(0, 240)]).wait_recv()
        pp[p] = dot3(split(qa[p]), (wh[p], wl[p]))
        c_send(C_ANS + p, lambda i: pp.at[p, tile(i, 16)], lambda i: rc.at[p, tile(i, 16)])

    def summed(p):
        rc[p, tile(c, 16)] = pp[p, tile(c, 16)]
        c_all(C_ANS + p, rc.at[p, pl.ds(0, 240)]).wait_recv()
        return block_sum(rc.at[p], 16)

    lane = lax.broadcasted_iota(jnp.int32, (16, 128), 1)
    own_lanes = lane // 64 == k

    def swap(p):
        return k_copy(K_OUT + p, xb.at[p], xs.at[p])

    def share(p):
        swap(p).wait_recv()
        own = ob.at[p, tile(c, 16)]
        own[...] = jnp.where(own_lanes, xb[p], pltpu.roll(xs[p], 64, 1))
        c_send(C_OUT + p, lambda i: own, lambda i: ob.at[p, tile(i, 16)])

    lower(0)

    ru[tile(c, 32)] = pu[tile(c, 32)]
    c_all(C_U, ru.at[pl.ds(0, 480)]).wait_recv()
    own_u = ug.at[k, tile(c, 32)]
    own_u[...] = block_sum(ru, 32)
    c_send(C_UALL, lambda i: own_u, lambda i: ug.at[k, tile(i, 32)])

    own_a = ga.at[:, tile(z, 128)]
    answer_0 = summed(0)
    own_a[...] = answer_0
    z_send(Z_ANS, lambda i: own_a, lambda i: ga.at[:, tile(i, 128)])
    xb[0] = answer_0
    swap(0).start()

    c_all(C_UALL, ug.at[k, pl.ds(0, 480)]).wait_recv()
    half = ug.at[k]
    k_copy(K_U, half, half).start()
    lower(1)

    share(0)

    k_copy(K_U, half, ug.at[ok]).wait_recv()
    imag = lax.rem(lax.broadcasted_iota(jnp.int32, (32, 128), 1) // 32, 2) == 1

    def weigh(i, _):
        for q in range(2):
            v = ug[q, tile(i, 32)]
            v2 = jnp.where(imag, pltpu.roll(v, 32, 1), -pltpu.roll(v, 96, 1))
            hi, lo = split(jnp.concatenate([v, v2], axis=0))
            ubh[tile(place(i) * 2 + q, 64)] = hi
            ubl[tile(place(i) * 2 + q, 64)] = lo
        return 0

    lax.fori_loop(0, NC, weigh, 0)
    own_1 = summed(1)

    z_all(Z_ANS, ga.at[:, pl.ds(0, 15 * 128)]).wait_recv()
    hi, lo = split(ga[...])
    first = jnp.dot(jnp.concatenate([hi, lo], 0), ubh[...], preferred_element_type=F32)
    xb[1] = own_1 - (first[:16] + (first[16:] + jnp.dot(hi, ubl[...], preferred_element_type=F32)))
    swap(1).start()
    share(1)

    for p in range(2):
        c_all(C_OUT + p, ob.at[p, pl.ds(0, 240)]).wait_recv()
        turned = ob[p].T
        for h in range(2):
            for s in range(2):
                at = (h * 2 + s) * 32
                o_ref[s, p, :, pl.ds(h * 256, 256)] = turned[at : at + 32]

    z_all(Z_PRIOR, rb.at[pl.ds(0, 240)]).wait_send()
    z_all(Z_NEAR, ra).wait_send()
    z_all(Z_CPL, cg.at[pl.ds(0, 96)]).wait_send()
    z_all(Z_CPL2, cg.at[pl.ds(0, 384)]).wait_send()
    z_all(Z_FOURTH, rf.at[pl.ds(1, 3)]).wait_send()
    z_all(Z_ANS, ga.at[:, pl.ds(0, 15 * 128)]).wait_send()
    c_all(C_U, ru.at[pl.ds(0, 480)]).wait_send()
    c_all(C_UALL, ug.at[k, pl.ds(0, 480)]).wait_send()
    for p in range(2):
        z_all(Z_Q + p, qa.at[p, pl.ds(0, 240)]).wait_send()
        c_all(C_ANS + p, rc.at[p, pl.ds(0, 240)]).wait_send()
        c_all(C_OUT + p, ob.at[p, pl.ds(0, 240)]).wait_send()
    k_copy(0, cx.at[0], cx.at[0]).wait_send()
    k_copy(1, cx.at[1], cx.at[1]).wait_send()
    k_copy(K_INV, own_d, own_d).wait_send()
    k_copy(K_U, half, half).wait_send()
    for p in range(2):
        swap(p).wait_send()


def per_device(solved, upper_cols, coupling, inverse_diag, right_side):
    vmem = pl.BlockSpec(memory_space=pltpu.VMEM)
    hbm = pl.BlockSpec(memory_space=pltpu.HBM)
    f = lambda *shape: pltpu.VMEM(shape, F32)
    b = lambda *shape: pltpu.VMEM(shape, BF16)
    return pl.pallas_call(
        kernel,
        out_shape=pltpu.VMEM((2, 2, 32, 512), F32),
        in_specs=[hbm] * 5,
        out_specs=vmem,
        scratch_shapes=[
            f(2, 2, 2, 32, 64), f(2, 32, 64), f(256, 1024), f(2, 1024, 512), f(2, 256, 512), f(2, 512, 128),
            f(2, 256, 128), f(2, 256, 128), f(256, 128), f(192, 128), f(64, 128), f(4, 16, 128), f(2, 128, 128), f(2, 128, 128),
            b(2, 128, 128), b(2, 128, 128), f(2, 256, 128), f(512, 128), f(512, 128), f(512, 128), f(2, 512, 128),
            b(2048, 128), b(2048, 128), f(2, 256, 128), f(2, 256, 128), f(16, 2048), f(2, 16, 128), f(2, 16, 128),
            f(2, 256, 128),
            pltpu.SemaphoreType.DMA((18,)),
            pltpu.SemaphoreType.DMA((8,)), pltpu.SemaphoreType.DMA((8,)),
            pltpu.SemaphoreType.DMA((6,)), pltpu.SemaphoreType.DMA((6,)),
            pltpu.SemaphoreType.DMA((6,)), pltpu.SemaphoreType.DMA((6,)),
        ],
        compiler_params=pltpu.CompilerParams(
            collective_id=0, has_side_effects=True, vmem_limit_bytes=VMEM
        ),
        name="panels",
    )(solved, upper_cols, right_side, inverse_diag, jnp.swapaxes(coupling, 1, 2))


def solution(mesh):
    in_specs = (
        P(None, "row", None),
        P(None, None, "col", "row"),
        P(None, "col", "row"),
        P(None, None, "row", "col"),
        P(None, None, "col", None),
    )
    out_specs = P(None, None, "row", None)
    return jax.shard_map(
        per_device, mesh=mesh, in_specs=in_specs, out_specs=out_specs, check_vma=False
    )
```
